256 devices in a mesh: stream: 8 (over z), girth: 8 (over x, core), prop: 4 (over y).
Axes of the slice: x: 4, y: 4, z: 8, core: 2. Of those that a mesh axis runs over, the one named last changes fastest.
Arguments:
- velocity: float32 [3, 64, 128, 1024], P(None, 'stream', 'girth', 'prop'), may hold values from -6 to 6
- eddy_visc: float32 [64, 128, 1024], P('stream', 'girth', 'prop'), may hold values from 0.05 to 0.5
- solid: int32 [64, 128, 1024], P('stream', 'girth', 'prop'), may hold values 0 or 1
- pressure_old: float32 [64, 128, 1024], P('stream', 'girth', 'prop'), may hold values from -6 to 6
- relaxation: float32 [64, 128, 1024], P('stream', 'girth', 'prop'), may hold values from 0.05 to 0.5
- host_cell: int32 [3, 1024], replicated, may hold values from 0 to 1022, as said below
- offsets: float32 [3, 1024], replicated, may hold values from 0 to 1
- blade_motion: float32 [3, 1024], replicated, may hold values from -12 to 12
- force_coeff: float32 [1024], replicated, may hold values from 0.05 to 0.5
Outputs:
- velocity_new: float32 [3, 64, 128, 1024], P(None, 'stream', 'girth', 'prop')
- pressure: float32 [64, 128, 1024], P('stream', 'girth', 'prop')
- blade_velocity: float32 [3, 1024], replicated
The draws below stay inside these ranges and needn't reach their ends.
Inputs may be any that keep to these rules, and one draw needn't show every extreme that they name: host_cell[0] lies in 31 to 33; host_cell[1] lies in 0 to 126 and host_cell[2] in 0 to 1022, so that all 8 corners are inside the grid.
All inputs are finite; a program needn't handle non-finite values. No bound on the sum of `solid` on one device may be relied on, other than what follows from the above.
Results may differ from the reference program's by a relative error of at most 0.0001.
Values sent between devices are 32-bit elements; how exact they have to be, the bound alone decides.
No kernel may reach another device: no remote copies, remote signals or barrier semaphores. Data moves between devices by JAX's collectives and lax.ppermute only.
A program may use at most 128 MiB of HBM per device.

```python
import math
import jax
import jax.numpy as jnp
from jax import lax

CG_ITERS = 2
POINTS = 1024
NX = 64
NY = 128
NZ = 1024


def draw_host_cell(key, part):
    key_x = jax.random.fold_in(key, 11)
    key_y = jax.random.fold_in(key, 12)
    key_z = jax.random.fold_in(key, 13)
    key_cy = jax.random.fold_in(key, 14)
    key_cz = jax.random.fold_in(key, 15)
    centre_y = jax.random.randint(key_cy, (), 0, NY - 3)
    centre_z = jax.random.randint(key_cz, (), 0, NZ - 3)
    coord_x = NX // 2 - 1 + jax.random.randint(key_x, (POINTS,), 0, 3)
    coord_y = centre_y + jax.random.randint(key_y, (POINTS,), 0, 3)
    coord_z = centre_z + jax.random.randint(key_z, (POINTS,), 0, 3)
    coord_y = coord_y.at[0].set(0).at[POINTS - 1].set(NY - 2)
    coord_z = coord_z.at[0].set(0).at[POINTS - 1].set(NZ - 2)
    return jnp.stack([coord_x, coord_y, coord_z]).astype(jnp.int32)


def set_ends(values, own_key, least, high):
    dims = values.shape
    index_at = [jax.random.randint(jax.random.fold_in(own_key, axis), (), 0, dims[axis]) for axis in range(len(dims))]
    values = values.at[tuple(index_at)].set(least)
    longest = dims.index(max(dims))
    index_at[longest] = (index_at[longest] + 1) % dims[longest]
    return values.at[tuple(index_at)].set(high)


def level_of(stream_key, dims, pieces, least, largest):
    def one(position, shards_of):
        draws = jax.random.uniform(jax.random.fold_in(jax.random.fold_in(stream_key, 6), position), (shards_of,), jnp.float32, least / len(pieces), largest / len(pieces))
        return jnp.repeat(jnp.exp(draws), dims[position] // shards_of).reshape((-1,) + (1,) * (len(dims) - position - 1))

    factor_of = one(*pieces[0])
    for cut in pieces[1:]:
        factor_of = factor_of * one(*cut)
    return factor_of


def noise(key, shape, deviation, most, split=(), dtype=jnp.bfloat16):
    entries = deviation * jax.random.normal(key, shape, jnp.float32)
    if split:
        entries = entries * level_of(key, shape, split, -0.22, 0.18)
    return jnp.clip(entries, -most, most).astype(dtype)


def setup_inputs(seed: int = 0) -> dict:
    key_of = jax.random.split(jax.random.key(seed), 10)
    velocity = noise(key_of[0], (3, NX, NY, NZ), 1.0, 6.0, ((1, 8), (2, 8), (3, 4)), jnp.float32)
    eddy_visc = jnp.clip(jnp.exp(math.log(0.5) - 2.3025851 * jax.random.uniform(key_of[1], (NX, NY, NZ), jnp.float32) ** level_of(key_of[1], (NX, NY, NZ), ((0, 8), (1, 8), (2, 4)), -0.2, 0.2)), 0.05, 0.5)
    solid = set_ends((jax.random.randint(key_of[2], (NX, NY, NZ), 0, 8) < 1).astype(jnp.int32), jax.random.fold_in(key_of[2], 1), 0, 1)
    pressure_old = noise(key_of[3], (NX, NY, NZ), 1.0, 6.0, ((0, 8), (1, 8), (2, 4)), jnp.float32)
    relaxation = jnp.clip(jnp.exp(math.log(0.5) - 2.3025851 * jax.random.uniform(key_of[4], (NX, NY, NZ), jnp.float32) ** level_of(key_of[4], (NX, NY, NZ), ((0, 8), (1, 8), (2, 4)), -0.2, 0.2)), 0.05, 0.5)
    host_cell = draw_host_cell(jax.random.fold_in(key_of[9], 71), 0)
    offsets = jnp.clip(jax.random.uniform(key_of[6], (3, POINTS), jnp.float32, 0.0, 1.0), 0.0, 1.0)
    blade_motion = noise(key_of[7], (3, POINTS), 2.0, 12.0, (), jnp.float32)
    force_coeff = jnp.clip(jnp.exp(jax.random.uniform(key_of[8], (POINTS,), jnp.float32, math.log(0.05), math.log(0.5))), 0.05, 0.5)
    return dict(velocity=velocity, eddy_visc=eddy_visc, solid=solid, pressure_old=pressure_old, relaxation=relaxation, host_cell=host_cell, offsets=offsets, blade_motion=blade_motion, force_coeff=force_coeff)


DT = 0.1

def shifted(field):
    padded = jnp.pad(field, 1)
    plus = [padded[2:, 1:-1, 1:-1], padded[1:-1, 2:, 1:-1], padded[1:-1, 1:-1, 2:]]
    minus = [padded[:-2, 1:-1, 1:-1], padded[1:-1, :-2, 1:-1], padded[1:-1, 1:-1, :-2]]
    return (plus, minus)

def operate(field, relaxation):
    plus, minus = shifted(field)
    return (6.0 + relaxation) * field - (plus[0] + minus[0] + plus[1] + minus[1] + plus[2] + minus[2])

def reference(velocity, eddy_visc, solid, pressure_old, relaxation, host_cell, offsets, blade_motion, force_coeff):
    keep = 1.0 - solid.astype(jnp.float32)
    parts = [shifted(velocity[k]) for k in range(3)]
    predicted = []
    for k in range(3):
        plus, minus = parts[k]
        lap = plus[0] + minus[0] + plus[1] + minus[1] + plus[2] + minus[2] - 6.0 * velocity[k]
        conv = sum((velocity[d] * (plus[d] - minus[d]) * 0.5 for d in range(3)))
        predicted.append(keep * (velocity[k] + DT * (eddy_visc * lap - conv)))
    div = jnp.zeros_like(eddy_visc)
    for d in range(3):
        plus, minus = shifted(predicted[d])
        div = div + (plus[d] - minus[d]) * 0.5
    source = -div / DT
    pressure = pressure_old
    residual = source - operate(pressure_old, relaxation)
    direction = residual
    rr = jnp.sum(residual * residual)
    for step in range(CG_ITERS):
        image = operate(direction, relaxation)
        alpha = rr / jnp.sum(direction * image)
        pressure = pressure + alpha * direction
        residual = residual - alpha * image
        new = jnp.sum(residual * residual)
        direction = residual + new / rr * direction
        rr = new
    plus, minus = shifted(pressure)
    corrected = jnp.stack([keep * (predicted[d] - DT * (plus[d] - minus[d]) * 0.5) for d in range(3)])
    point_vel = jnp.zeros((3, POINTS), jnp.float32)
    corners = []
    for a in range(2):
        for b in range(2):
            for c in range(2):
                weight = jnp.ones((POINTS,), jnp.float32)
                for d, bit in enumerate((a, b, c)):
                    weight = weight * (offsets[d] if bit else 1.0 - offsets[d])
                gx = host_cell[0] + a
                gy = host_cell[1] + b
                gz = host_cell[2] + c
                corners.append((gx, gy, gz, weight))
                point_vel = point_vel + corrected[:, gx, gy, gz] * weight[None, :]
    slip = point_vel - blade_motion
    speed = jnp.sqrt(lax.optimization_barrier(jnp.sum(slip * slip, axis=0)) + 1.0)
    point_force = -force_coeff[None, :] * speed[None, :] * slip
    body_force = jnp.zeros_like(corrected)
    for gx, gy, gz, weight in corners:
        body_force = body_force.at[:, gx, gy, gz].add(point_force * weight[None, :])
    velocity_new = corrected + DT * body_force
    return (velocity_new, pressure, point_vel)
```

```python
import jax
import jax.numpy as jnp
from jax import lax
from jax.experimental import pallas as pl
from jax.experimental.pallas import tpu as pltpu
from jax.sharding import PartitionSpec as P

DT = 0.1
F32 = jnp.float32
AXES = ("stream", "girth", "prop")

X, Y, Z = 8, 16, 256
YE, ZE = 24, 384
RADIUS = (4, 4, 4, 3, 3, 3, 2)
XOFF = (0, 4, 8, 12, 15, 18, 21)
XLAYERS = 23
BASE = (0, 16, 32, 48, 62, 76, 90)
LAYERS = 102
VISC, KEEP, PRES, RELAX = 3, 4, 5, 6
YLAYERS = [(f, x) for f in range(7) for x in range(1 - RADIUS[f], X - 1 + RADIUS[f])]
YPAIRS = len(YLAYERS) // 2
YUNITS = -(-YPAIRS // 16)
YTILES = YPAIRS + -(-YUNITS // 2)
WINDOW = 3
VMEM = pl.BlockSpec(memory_space=pltpu.VMEM)
PARAMS = pltpu.CompilerParams(vmem_limit_bytes=48 * 1024 * 1024)


def iota(shape, dim):
    return lax.broadcasted_iota(jnp.int32, shape, dim)


def roll(a, shift, axis):
    shift = shift % a.shape[axis]
    return a if shift == 0 else pltpu.roll(a, shift, axis)


def own_layer(refs, f, x):
    if f < 3:
        return refs[0][f, x]
    if f == KEEP:
        return 1.0 - refs[2][x].astype(F32)
    return refs[{VISC: 1, PRES: 3, RELAX: 4}[f]][x]


def pack_kernel(*args):
    refs, (up, down, z_up, z_down, uu, ud, du, dd) = args[:5], args[5:]
    for f, (r, off) in enumerate(zip(RADIUS, XOFF)):
        for i in range(r):
            up[off + i] = own_layer(refs, f, X - r + i)
            down[off + i] = own_layer(refs, f, i)
    slot = iota((Y, 128), 1) // 4

    def pack(layers, to_up, to_down):
        high = jnp.zeros((Y, 128), F32)
        low = jnp.zeros((Y, 128), F32)
        for j, layer in enumerate(layers):
            high = jnp.where(slot == j, roll(layer[:, Z - 128 :], 4 * j - 124, 1), high)
            low = jnp.where(slot == j, roll(layer[:, :128], 4 * j, 1), low)
        to_up[...] = high
        to_down[...] = low

    every = [(f, x) for f in range(7) for x in range(X)]
    for unit in range(2):
        pack(
            [own_layer(refs, f, x) for f, x in every[unit * 32 : unit * 32 + 32]],
            z_up.at[unit],
            z_down.at[unit],
        )
    tops = [(f, X - RADIUS[f] + i) for f in range(7) for i in range(RADIUS[f])]
    lows = [(f, i) for f in range(7) for i in range(RADIUS[f])]
    pack([own_layer(refs, f, x) for f, x in tops], uu, ud)
    pack([own_layer(refs, f, x) for f, x in lows], du, dd)


def inside_flags():
    out = []
    for axis in AXES:
        i = lax.axis_index(axis)
        out.append((i > 0).astype(F32))
        out.append((i < lax.axis_size(axis) - 1).astype(F32))
    return out


def layer_reader(refs, got):
    xm, xp, zm, zp, mm, mp, pm, pp = got
    in_xm, in_xp, _, _, in_zm, in_zp = inside_flags()
    lane = iota((Y, 128), 1)
    right = (lane < 4).astype(F32) * in_zp
    left = (lane >= 124).astype(F32) * in_zm

    def third(minus, plus, j):
        return roll(plus, -4 * j, 1) * right + roll(minus, 124 - 4 * j, 1) * left

    def layer(f, x):
        r = RADIUS[f]
        if x < 0:
            i = XOFF[f] + x + r
            return xm[i] * in_xm, third(mm[...], mp[...], i) * in_xm
        if x >= X:
            i = XOFF[f] + x - X
            return xp[i] * in_xp, third(pm[...], pp[...], i) * in_xp
        q = f * X + x
        return own_layer(refs, f, x), third(zm[q // 32], zp[q // 32], q % 32)

    return layer


def edge_kernel(*args):
    refs, got, (to_up, to_down) = args[:5], args[5:13], args[13:]
    layer = layer_reader(refs, got)
    low_rows = iota((8, 128), 0) < 4
    slot = iota((8, 128), 1) // 8
    highs = [jnp.zeros((8, 128), F32) for _ in range(2 * (YTILES - YPAIRS))]
    lows = list(highs)

    def pair(a, b):
        high = jnp.where(low_rows, roll(a[8:], 4, 0), b[8:])
        low = jnp.where(low_rows, a[:8], roll(b[:8], 4, 0))
        return high, low

    for t in range(YPAIRS):
        a, a3 = layer(*YLAYERS[2 * t])
        b, b3 = layer(*YLAYERS[2 * t + 1])
        for half in range(2):
            cut = slice(128 * half, 128 * half + 128)
            to_up[t, :, cut], to_down[t, :, cut] = pair(a[:, cut], b[:, cut])
        high, low = pair(a3, b3)
        unit, j = t // 16, t % 16
        highs[unit] = jnp.where(slot == j, roll(high, 8 * j + 4, 1), highs[unit])
        lows[unit] = jnp.where(slot == j, roll(low, 8 * j + 4, 1), lows[unit])
    for t in range(YPAIRS, YTILES):
        for half in range(2):
            cut = slice(128 * half, 128 * half + 128)
            to_up[t, :, cut] = highs[2 * (t - YPAIRS) + half]
            to_down[t, :, cut] = lows[2 * (t - YPAIRS) + half]


def y_plus(a):
    return roll(a, -1, 0)


def y_minus(a):
    return roll(a, 1, 0)


def z_plus(a):
    return roll(a, -1, 1)


def z_minus(a):
    return roll(a, 1, 1)


def own(a):
    return a[:Y, :Z]


def main_kernel(*args):
    refs, got = args[:5], args[5:13]
    ym, yp, host, off, payload, grads, r0_out, s_out, ext, pred, res, img = args[13:]
    layer = layer_reader(refs, got)
    in_xm, in_xp, in_ym, in_yp, in_zm, in_zp = inside_flags()

    low_rows = iota((8, 128), 0) < 4
    lane = iota((8, 128), 1)
    ends = ((lane < 4) | (lane >= 124)).astype(F32)
    zero = jnp.zeros((8, 128), F32)
    place = {key: m for m, key in enumerate(YLAYERS)}
    for f in range(7):
        for x in range(-RADIUS[f], X + RADIUS[f]):
            at = BASE[f] + x + RADIUS[f]
            base, third = layer(f, x)
            ext[at, :Y, :Z] = base
            ext[at, :Y, Z:] = third
            m = place.get((f, x))
            if m is None:
                for half in range(3):
                    ext[at, Y:, 128 * half : 128 * half + 128] = zero
                continue
            t, odd = divmod(m, 2)

            def rows(plus, minus):
                plus, minus = plus * in_yp, minus * in_ym
                if odd:
                    return jnp.where(low_rows, roll(plus, 4, 0), minus)
                return jnp.where(low_rows, plus, roll(minus, 4, 0))

            for half in range(2):
                cut = slice(128 * half, 128 * half + 128)
                ext[at, Y:, cut] = rows(yp[t, :, cut], ym[t, :, cut])
            unit, j = divmod(t, 16)
            cut = slice(128 * (unit % 2), 128 * (unit % 2) + 128)
            last = YPAIRS + unit // 2
            packed = rows(yp[last, :, cut], ym[last, :, cut])
            ext[at, Y:, Z:] = roll(packed, -8 * j - 4, 1) * ends

    row, col = iota((YE, ZE), 0), iota((YE, ZE), 1)
    in_y = jnp.where(row < Y, 1.0, jnp.where(row < Y + 4, in_yp, in_ym))
    in_z = jnp.where(
        col < Z, 1.0, jnp.where(col < Z + 4, in_zp, jnp.where(col >= ZE - 4, in_zm, 0.0))
    )
    mask = in_y * in_z

    def field(f, x):
        return ext[BASE[f] + RADIUS[f] + x]

    def in_x(x):
        return jnp.where(x < 0, in_xm, jnp.where(x >= X, in_xp, 1.0))

    def predict(i, carry):
        x = i - 3
        speed = [field(d, x) for d in range(3)]
        visc, keep = field(VISC, x), field(KEEP, x)
        for k in range(3):
            center = speed[k]
            xp, xm = field(k, x + 1), field(k, x - 1)
            yp_, ym_ = y_plus(center), y_minus(center)
            zp_, zm_ = z_plus(center), z_minus(center)
            lap = xp + xm + yp_ + ym_ + zp_ + zm_ - 6.0 * center
            conv = 0.5 * (
                speed[0] * (xp - xm) + speed[1] * (yp_ - ym_) + speed[2] * (zp_ - zm_)
            )
            pred[k, i] = keep * (center + DT * (visc * lap - conv))
        return carry

    lax.fori_loop(0, X + 6, predict, 0)

    def residual(x, interior):
        div = 0.5 * (
            pred[0, x + 4]
            - pred[0, x + 2]
            + (y_plus(pred[1, x + 3]) - y_minus(pred[1, x + 3]))
            + (z_plus(pred[2, x + 3]) - z_minus(pred[2, x + 3]))
        )
        center = field(PRES, x)
        xp, xm = field(PRES, x + 1), field(PRES, x - 1)
        yp_, ym_ = y_plus(center), y_minus(center)
        zp_, zm_ = z_plus(center), z_minus(center)
        image = (6.0 + field(RELAX, x)) * center - (xp + xm + yp_ + ym_ + zp_ + zm_)
        value = (-div / DT - image) * (mask * in_x(x))
        res[x + 2] = value
        if interior:
            keep = own(field(KEEP, x))
            for d, (p, m) in enumerate(((xp, xm), (yp_, ym_), (zp_, zm_))):
                grads[d, x] = keep * (own(pred[d, x + 3]) - DT * 0.5 * (own(p) - own(m)))
            r0_out[x] = own(value)

    def image_of(x, interior):
        center = res[x + 2]
        xp, xm = res[x + 3], res[x + 1]
        yp_, ym_ = y_plus(center), y_minus(center)
        zp_, zm_ = z_plus(center), z_minus(center)
        value = (6.0 + field(RELAX, x)) * center - (xp + xm + yp_ + ym_ + zp_ + zm_)
        value = value * (mask * in_x(x))
        img[x + 1] = value
        if interior:
            keep = own(field(KEEP, x)) * (-DT * 0.5)
            for d, (p, m) in enumerate(((xp, xm), (yp_, ym_), (zp_, zm_))):
                grads[3 + d, x] = keep * (own(p) - own(m))
            s_out[x] = own(value)

    for x in (-2, -1, X, X + 1):
        residual(x, False)
    for x in range(X):
        residual(x, True)
    for x in (-1, X):
        image_of(x, False)
    for x in range(X):
        image_of(x, True)
    sums = [jnp.zeros((Y, Z), F32) for _ in range(4)]
    for x in range(X):
        center = img[x + 1]
        xp, xm = img[x + 2], img[x]
        yp_, ym_ = y_plus(center), y_minus(center)
        zp_, zm_ = z_plus(center), z_minus(center)
        nearby = own(xp) + own(xm) + own(yp_) + own(ym_) + own(zp_) + own(zm_)
        s, r = own(center), own(res[x + 2])
        image = (6.0 + own(field(RELAX, x))) * s - nearby
        keep = own(field(KEEP, x)) * (-DT * 0.5)
        for d, (p, m) in enumerate(((xp, xm), (yp_, ym_), (zp_, zm_))):
            grads[6 + d, x] = keep * (own(p) - own(m))
        for i, (a, b) in enumerate(((r, r), (r, s), (s, s), (s, image))):
            sums[i] = sums[i] + a * b
    payload[9] = jnp.zeros((8, 128), F32)
    for i, total in enumerate(sums):
        line = jnp.sum(total[:, :128] + total[:, 128:], axis=0, keepdims=True)
        payload[9, i : i + 1] = line

    first = window_start()
    samples = grads[:, pl.ds(first, WINDOW)].reshape(9 * WINDOW * Y, Z)
    width = 256
    for c in range(host.shape[1] // width):
        cut = slice(c * width, c * width + width)
        z_weights, xy_weights = point_weights(host, off, cut, first)
        parts = lax.dot_general(
            samples,
            z_weights,
            (((1,), (0,)), ((), ())),
            precision=lax.Precision.HIGHEST,
            preferred_element_type=F32,
        ).reshape(9, WINDOW, Y, width)
        for k in range(9):
            total = parts[k, 0] * xy_weights[0]
            for l in range(1, WINDOW):
                total = total + parts[k, l] * xy_weights[l]
            line = jnp.sum(total, axis=0, keepdims=True)
            for half in range(width // 128):
                at = c * (width // 128) + half
                payload[k, at : at + 1] = line[:, half * 128 : half * 128 + 128]


def window_start():
    return jnp.where(lax.axis_index("stream") * X + X == 32, X - WINDOW, 0)


def axis_weights(host, off, d, cut, place):
    low = host[d : d + 1, cut]
    part = off[d : d + 1, cut]
    return jnp.where(place == low, 1.0 - part, 0.0) + jnp.where(place == low + 1, part, 0.0)


def point_weights(host, off, cut, first):
    width = cut.stop - cut.start
    z_place = iota((Z, width), 0) + lax.axis_index("prop") * Z
    y_place = iota((Y, width), 0) + lax.axis_index("girth") * Y
    z_weights = axis_weights(host, off, 2, cut, z_place)
    y_weights = axis_weights(host, off, 1, cut, y_place)
    x_first = lax.axis_index("stream") * X + first
    xy = [y_weights * axis_weights(host, off, 0, cut, x_first + l) for l in range(WINDOW)]
    return z_weights, xy


def final_kernel(
    total, grads, pres, r0, s, host, off, motion, coeff, velocity, pressure, points, force
):
    lines = total[9]
    rr, rs, ss, st = [jnp.sum(lines[i : i + 1], axis=1, keepdims=True) for i in range(4)]
    alpha = rr / rs
    new = rr - 2.0 * alpha * rs + alpha * alpha * ss
    beta = new / rr
    grow = 1.0 + beta
    curve = grow * grow * rs - 2.0 * grow * alpha * ss + alpha * alpha * st
    alpha2 = new / curve
    c0 = alpha + alpha2 * grow
    c1 = -alpha2 * alpha
    for k in range(3):
        value = total[k] + c0 * total[3 + k] + c1 * total[6 + k]
        for i in range(8):
            points[k : k + 1, i * 128 : i * 128 + 128] = value[i : i + 1]
    slip = points[...] - motion[...]
    speed = jnp.sqrt(jnp.sum(slip * slip, axis=0, keepdims=True) + 1.0)
    force[...] = (-DT * coeff[...] * speed) * slip
    for x in range(X):
        pressure[x] = pres[x] + c0 * r0[x] + c1 * s[x]
        for k in range(3):
            velocity[k, x] = grads[k, x] + c0 * grads[3 + k, x] + c1 * grads[6 + k, x]
    first = window_start()
    width = 256
    body = jnp.zeros((3 * WINDOW * Y, Z), F32)
    for c in range(host.shape[1] // width):
        cut = slice(c * width, c * width + width)
        z_weights, xy_weights = point_weights(host, off, cut, first)
        scaled = jnp.concatenate(
            [xy_weights[l] * force[k : k + 1, cut] for k in range(3) for l in range(WINDOW)],
            axis=0,
        )
        body = body + lax.dot_general(
            scaled,
            z_weights,
            (((1,), (1,)), ((), ())),
            precision=lax.Precision.HIGHEST,
            preferred_element_type=F32,
        )
    body = body.reshape(3, WINDOW, Y, Z)
    for k in range(3):
        for l in range(WINDOW):
            velocity[k, first + l] = velocity[k, first + l] + body[k, l]


def shift(value, steps):
    names = tuple(steps)
    sizes = [lax.axis_size(n) for n in names]
    if len(names) == 1:
        n = sizes[0]
        moves = [(i, (i + steps[names[0]]) % n) for i in range(n)]
        return lax.ppermute(value, names[0], moves)
    moves = []
    for i in range(sizes[0]):
        for j in range(sizes[1]):
            to = ((i + steps[names[0]]) % sizes[0]) * sizes[1] + (j + steps[names[1]]) % sizes[1]
            moves.append((i * sizes[1] + j, to))
    return lax.ppermute(value, names, moves)


def total_over(value, axis):
    n = lax.axis_size(axis)
    copies = jnp.broadcast_to(value[None], (n,) + value.shape)
    return jnp.sum(lax.all_to_all(copies, axis, 0, 0), axis=0)


def sds(*shape):
    return jax.ShapeDtypeStruct(shape, F32)


def call(kernel, outs, inputs, scratch=(), name=None):
    return pl.pallas_call(
        kernel,
        out_shape=outs,
        in_specs=[VMEM] * len(inputs),
        out_specs=[VMEM] * len(outs),
        scratch_shapes=scratch,
        compiler_params=PARAMS,
        name=name,
    )(*inputs)


def shards(
    velocity, eddy_visc, solid, pressure_old, relaxation, host_cell, offsets, blade_motion, force_coeff
):
    fields = (velocity, eddy_visc, solid, pressure_old, relaxation)
    points = host_cell.shape[1]
    side, unit = sds(XLAYERS, Y, Z), sds(Y, 128)
    up, down, z_up, z_down, uu, ud, du, dd = call(
        pack_kernel,
        (side, side, sds(2, Y, 128), sds(2, Y, 128), unit, unit, unit, unit),
        fields,
        name="pack",
    )
    got = (
        shift(up, {"stream": 1}),
        shift(down, {"stream": -1}),
        shift(z_up, {"prop": 1}),
        shift(z_down, {"prop": -1}),
        shift(uu, {"stream": 1, "prop": 1}),
        shift(ud, {"stream": 1, "prop": -1}),
        shift(du, {"stream": -1, "prop": 1}),
        shift(dd, {"stream": -1, "prop": -1}),
    )
    edge = sds(YTILES, 8, Z)
    y_up, y_down = call(edge_kernel, (edge, edge), fields + got, name="edges")
    ym, yp = shift(y_up, {"girth": 1}), shift(y_down, {"girth": -1})
    block = sds(X, Y, Z)
    payload, grads, r0, s = call(
        main_kernel,
        (sds(10, 8, 128), sds(9, X, Y, Z), block, block),
        fields + got + (ym, yp, host_cell, offsets),
        [
            pltpu.VMEM((LAYERS, YE, ZE), F32),
            pltpu.VMEM((3, X + 6, YE, ZE), F32),
            pltpu.VMEM((X + 4, YE, ZE), F32),
            pltpu.VMEM((X + 2, YE, ZE), F32),
        ],
        name="main",
    )
    total = payload
    for axis in ("girth", "prop", "stream"):
        total = total_over(total, axis)
    return call(
        final_kernel,
        (sds(3, X, Y, Z), block, sds(3, points)),
        (
            total,
            grads,
            pressure_old,
            r0,
            s,
            host_cell,
            offsets,
            blade_motion,
            force_coeff.reshape(1, points),
        ),
        [pltpu.VMEM((3, points), F32)],
        name="final",
    )


def solution(mesh):
    placed = (P(None, *AXES),) + (P(*AXES),) * 4 + (P(),) * 4
    return jax.shard_map(
        shards,
        mesh=mesh,
        in_specs=placed,
        out_specs=(P(None, *AXES), P(*AXES), P()),
        check_vma=False,
    )
```

```python
import jax
import jax.numpy as jnp
from jax import lax
from jax.experimental import pallas as pl
from jax.experimental.pallas import tpu as pltpu
from jax.sharding import Mesh, PartitionSpec as P

DT = 0.1
F32 = jnp.float32

X, Y, Z = 8, 16, 256
YE, ZE = 24, 384
VISC, KEEP, PRES, RELAX = 3, 4, 5, 6
FIELDS = 7
RADIUS = (4, 3, 3, 3, 3, 3, 2)
XLAYERS = [(f, d) for f in range(FIELDS) for d in range(1, RADIUS[f] + 1)]
CORNER = (3, 3, 3, 2, 2, 2, 1)
RELAYED = [(f, d) for f in range(FIELDS) for d in range(1, CORNER[f] + 1)]
YPAIRS = FIELDS * X // 2
YTILES = YPAIRS + 1
RTILES = len(RELAYED) + 2
WINDOW = 3
VMEM = pl.BlockSpec(memory_space=pltpu.VMEM)
PARAMS = pltpu.CompilerParams(vmem_limit_bytes=48 * 1024 * 1024)


def iota(shape, dim):
    return lax.broadcasted_iota(jnp.int32, shape, dim)


def roll(a, shift, axis):
    shift = shift % a.shape[axis]
    return a if shift == 0 else pltpu.roll(a, shift, axis)


def halves(width=Z):
    return [slice(i, i + 128) for i in range(0, width, 128)]


def pack_kernel(
    velocity, visc, solid, pres, relax, own_out, up, down, z_up, z_down, stage, sems
):
    copies = [
        pltpu.make_async_copy(velocity, own_out.at[:3], sems.at[0]),
        pltpu.make_async_copy(visc, own_out.at[VISC], sems.at[1]),
        pltpu.make_async_copy(solid, stage, sems.at[2]),
        pltpu.make_async_copy(pres, own_out.at[PRES], sems.at[3]),
        pltpu.make_async_copy(relax, own_out.at[RELAX], sems.at[4]),
    ]
    for copy in copies:
        copy.start()
    for copy in copies:
        copy.wait()
    own_out[KEEP] = 1.0 - stage[...].astype(F32)
    slot = iota((Y, 128), 1) // 4
    for unit in range(2):
        high = jnp.zeros((Y, 128), F32)
        low = jnp.zeros((Y, 128), F32)
        for j in range(32):
            q = unit * 32 + j
            if q < FIELDS * X:
                f, x = divmod(q, X)
                high = jnp.where(slot == j, roll(own_out[f, x, :, Z - 128 :], 4 * j - 124, 1), high)
                low = jnp.where(slot == j, roll(own_out[f, x, :, :128], 4 * j, 1), low)
        z_up[unit] = high
        z_down[unit] = low
    for i, (f, d) in enumerate(XLAYERS):
        up[i] = own_out[f, X - d]
        down[i] = own_out[f, d - 1]


def position():
    return (
        lax.axis_index("stream"),
        lax.axis_index("gx") * 2 + lax.axis_index("core"),
        lax.axis_index("prop"),
    )


def inside_flags():
    out = []
    for i, n in zip(position(), (8, 8, 4)):
        out.append((i > 0).astype(F32))
        out.append((i < n - 1).astype(F32))
    return out


def third_reader(zm, zp):
    in_zm, in_zp = inside_flags()[4:]
    lane = iota((Y, 128), 1)
    right = (lane < 4).astype(F32) * in_zp
    left = (lane >= 124).astype(F32) * in_zm

    def third(f, x):
        unit, j = divmod(f * X + x, 32)
        return roll(zp[unit], -4 * j, 1) * right + roll(zm[unit], 124 - 4 * j, 1) * left

    return third


def edge_kernel(fields, zm, zp, to_up, to_down):
    third = third_reader(zm, zp)
    low_rows = iota((8, 128), 0) < 4
    slot = iota((8, 128), 1) // 8
    highs = [jnp.zeros((8, 128), F32) for _ in range(2)]
    lows = [jnp.zeros((8, 128), F32) for _ in range(2)]

    def pair(a, b):
        high = jnp.where(low_rows, roll(a[8:], 4, 0), b[8:])
        low = jnp.where(low_rows, a[:8], roll(b[:8], 4, 0))
        return high, low

    for t in range(YPAIRS):
        f, x = divmod(2 * t, X)
        for cut in halves():
            to_up[t, :, cut], to_down[t, :, cut] = pair(fields[f, x, :, cut], fields[f, x + 1, :, cut])
        high, low = pair(third(f, x), third(f, x + 1))
        unit, j = divmod(t, 16)
        highs[unit] = jnp.where(slot == j, roll(high, 8 * j + 4, 1), highs[unit])
        lows[unit] = jnp.where(slot == j, roll(low, 8 * j + 4, 1), lows[unit])
    for unit, cut in enumerate(halves()):
        to_up[YPAIRS, :, cut] = highs[unit]
        to_down[YPAIRS, :, cut] = lows[unit]


def block_kernel(fields, zm, zp, ym, yp, ext, to_up, to_down):
    third = third_reader(zm, zp)
    _, _, in_ym, in_yp, _, _ = inside_flags()
    low_rows = iota((8, 128), 0) < 4
    slot = iota((8, 128), 1) // 8
    lane = iota((8, 128), 1)
    ends = ((lane < 4) | (lane >= 124)).astype(F32)

    def rows(t, cut, odd):
        plus, minus = yp[t, :, cut] * in_yp, ym[t, :, cut] * in_ym
        if odd:
            return jnp.where(low_rows, roll(plus, 4, 0), minus)
        return jnp.where(low_rows, plus, roll(minus, 4, 0))

    for f in range(FIELDS):
        for x in range(X):
            t, odd = divmod(f * X + x, 2)
            ext[f, x, :Y, :Z] = fields[f, x]
            ext[f, x, :Y, Z:] = third(f, x)
            for cut in halves():
                ext[f, x, Y:, cut] = rows(t, cut, odd)
            unit, j = divmod(t, 16)
            packed = rows(YPAIRS, halves()[unit], odd)
            ext[f, x, Y:, Z:] = roll(packed, -8 * j - 4, 1) * ends
    for up, out in ((True, to_up), (False, to_down)):
        units = [jnp.zeros((8, 128), F32) for _ in range(4)]
        for i, (f, d) in enumerate(RELAYED):
            x = X - d if up else d - 1
            out[i] = ext[f, x, Y:, :Z]
            for h in range(3):
                unit, j = divmod(3 * i + h, 16)
                tile = roll(ext[f, x, 8 * h : 8 * h + 8, Z:], 8 * j + 4, 1)
                units[unit] = jnp.where(slot == j, tile, units[unit])
        for unit in range(4):
            out[len(RELAYED) + unit // 2, :, halves()[unit % 2]] = units[unit]


def y_plus(a):
    return roll(a, -1, 0)


def y_minus(a):
    return roll(a, 1, 0)


def z_plus(a):
    return roll(a, -1, 1)


def z_minus(a):
    return roll(a, 1, 1)


def own(a):
    return a[:Y, :Z]


def main_kernel(
    ext, xm, xp, rm, rp, host, off, keep_half, send_half, grads, r0_out, s_out, *scratch
):
    halo, pred, res, img, payload = scratch
    in_xm, in_xp, in_ym, in_yp, in_zm, in_zp = inside_flags()

    lane = iota((8, 128), 1)
    ends = ((lane < 4) | (lane >= 124)).astype(F32)
    for side, (edge, relay, flag) in enumerate(((xm, rm, in_xm), (xp, rp, in_xp))):
        for i, layer in enumerate(XLAYERS):
            halo[side, i, :Y, :Z] = edge[i] * flag
            if layer not in RELAYED:
                halo[side, i, :Y, Z:] = jnp.zeros((Y, 128), F32)
                halo[side, i, Y:] = jnp.zeros((8, ZE), F32)
                continue
            n = RELAYED.index(layer)
            halo[side, i, Y:, :Z] = relay[n] * flag
            for h in range(3):
                unit, j = divmod(3 * n + h, 16)
                packed = relay[len(RELAYED) + unit // 2, :, halves()[unit % 2]]
                halo[side, i, 8 * h : 8 * h + 8, Z:] = roll(packed, -8 * j - 4, 1) * (ends * flag)

    row, col = iota((YE, ZE), 0), iota((YE, ZE), 1)
    in_y = jnp.where(row < Y, 1.0, jnp.where(row < Y + 4, in_yp, in_ym))
    in_z = jnp.where(
        col < Z, 1.0, jnp.where(col < Z + 4, in_zp, jnp.where(col >= ZE - 4, in_zm, 0.0))
    )
    mask = in_y * in_z

    def field(f, x):
        if x < 0:
            return halo[0, XLAYERS.index((f, -x))]
        if x >= X:
            return halo[1, XLAYERS.index((f, x - X + 1))]
        return ext[f, x]

    def in_x(x):
        return in_xm if x < 0 else in_xp if x >= X else 1.0

    for x in range(-3, X + 3):
        speed = [field(d, x) for d in range(3)]
        visc, keep = field(VISC, x), field(KEEP, x)
        for k in range(3 if -3 < x < X + 2 else 1):
            center = speed[k]
            xp_, xm_ = field(k, x + 1), field(k, x - 1)
            yp_, ym_ = y_plus(center), y_minus(center)
            zp_, zm_ = z_plus(center), z_minus(center)
            lap = xp_ + xm_ + yp_ + ym_ + zp_ + zm_ - 6.0 * center
            conv = 0.5 * (
                speed[0] * (xp_ - xm_) + speed[1] * (yp_ - ym_) + speed[2] * (zp_ - zm_)
            )
            pred[k, x + 3] = keep * (center + DT * (visc * lap - conv))

    def residual(x, interior):
        div = 0.5 * (
            pred[0, x + 4]
            - pred[0, x + 2]
            + (y_plus(pred[1, x + 3]) - y_minus(pred[1, x + 3]))
            + (z_plus(pred[2, x + 3]) - z_minus(pred[2, x + 3]))
        )
        center = field(PRES, x)
        xp, xm = field(PRES, x + 1), field(PRES, x - 1)
        yp_, ym_ = y_plus(center), y_minus(center)
        zp_, zm_ = z_plus(center), z_minus(center)
        image = (6.0 + field(RELAX, x)) * center - (xp + xm + yp_ + ym_ + zp_ + zm_)
        value = (-div / DT - image) * (mask * in_x(x))
        res[x + 2] = value
        if interior:
            keep = own(field(KEEP, x))
            for d, (p, m) in enumerate(((xp, xm), (yp_, ym_), (zp_, zm_))):
                grads[d, x] = keep * (own(pred[d, x + 3]) - DT * 0.5 * (own(p) - own(m)))
            r0_out[x] = own(value)

    def image_of(x, interior):
        center = res[x + 2]
        xp, xm = res[x + 3], res[x + 1]
        yp_, ym_ = y_plus(center), y_minus(center)
        zp_, zm_ = z_plus(center), z_minus(center)
        value = (6.0 + field(RELAX, x)) * center - (xp + xm + yp_ + ym_ + zp_ + zm_)
        value = value * (mask * in_x(x))
        img[x + 1] = value
        if interior:
            keep = own(field(KEEP, x)) * (-DT * 0.5)
            for d, (p, m) in enumerate(((xp, xm), (yp_, ym_), (zp_, zm_))):
                grads[3 + d, x] = keep * (own(p) - own(m))
            s_out[x] = own(value)

    for x in (-2, -1, X, X + 1):
        residual(x, False)
    for x in range(X):
        residual(x, True)
    for x in (-1, X):
        image_of(x, False)
    for x in range(X):
        image_of(x, True)
    sums = [jnp.zeros((Y, Z), F32) for _ in range(4)]
    for x in range(X):
        center = img[x + 1]
        xp, xm = img[x + 2], img[x]
        yp_, ym_ = y_plus(center), y_minus(center)
        zp_, zm_ = z_plus(center), z_minus(center)
        nearby = own(xp) + own(xm) + own(yp_) + own(ym_) + own(zp_) + own(zm_)
        s, r = own(center), own(res[x + 2])
        image = (6.0 + own(field(RELAX, x))) * s - nearby
        keep = own(field(KEEP, x)) * (-DT * 0.5)
        for d, (p, m) in enumerate(((xp, xm), (yp_, ym_), (zp_, zm_))):
            grads[6 + d, x] = keep * (own(p) - own(m))
        for i, (a, b) in enumerate(((r, r), (r, s), (s, s), (s, image))):
            sums[i] = sums[i] + a * b
    payload[9] = jnp.zeros((8, 128), F32)
    for i, total in enumerate(sums):
        line = jnp.sum(total[:, :128] + total[:, 128:], axis=0, keepdims=True)
        payload[9, i : i + 1] = line

    first = window_start()
    samples = grads[:, pl.ds(first, WINDOW)].reshape(9 * WINDOW * Y, Z)
    width = 256
    for c in range(host.shape[1] // width):
        cut = slice(c * width, c * width + width)
        z_weights, xy_weights = point_weights(host, off, cut, first)
        parts = lax.dot_general(
            samples,
            z_weights,
            (((1,), (0,)), ((), ())),
            precision=lax.Precision.HIGHEST,
            preferred_element_type=F32,
        ).reshape(9, WINDOW, Y, width)
        for k in range(9):
            total = parts[k, 0] * xy_weights[0]
            for l in range(1, WINDOW):
                total = total + parts[k, l] * xy_weights[l]
            line = jnp.sum(total, axis=0, keepdims=True)
            for half in range(width // 128):
                at = c * (width // 128) + half
                payload[k, at : at + 1] = line[:, half * 128 : half * 128 + 128]
    second = lax.axis_index("core") == 1
    for k in range(5):
        keep_half[k] = jnp.where(second, payload[5 + k], payload[k])
        send_half[k] = jnp.where(second, payload[k], payload[5 + k])


def window_start():
    return jnp.where(lax.axis_index("stream") * X + X == 32, X - WINDOW, 0)


def axis_weights(host, off, d, cut, place):
    low = host[d : d + 1, cut]
    part = off[d : d + 1, cut]
    return jnp.where(place == low, 1.0 - part, 0.0) + jnp.where(place == low + 1, part, 0.0)


def point_weights(host, off, cut, first):
    width = cut.stop - cut.start
    z_place = iota((Z, width), 0) + lax.axis_index("prop") * Z
    y_place = iota((Y, width), 0) + position()[1] * Y
    z_weights = axis_weights(host, off, 2, cut, z_place)
    y_weights = axis_weights(host, off, 1, cut, y_place)
    x_first = lax.axis_index("stream") * X + first
    xy = [y_weights * axis_weights(host, off, 0, cut, x_first + l) for l in range(WINDOW)]
    return z_weights, xy


def final_kernel(
    mine, other, fields, grads, r0, s, host, off, motion, coeff, velocity, pressure, points, force
):
    second = lax.axis_index("core") == 1
    total = [jnp.where(second, other[k], mine[k]) for k in range(5)]
    total += [jnp.where(second, mine[k], other[k]) for k in range(5)]
    lines = total[9]
    rr, rs, ss, st = [jnp.sum(lines[i : i + 1], axis=1, keepdims=True) for i in range(4)]
    alpha = rr / rs
    new = rr - 2.0 * alpha * rs + alpha * alpha * ss
    beta = new / rr
    grow = 1.0 + beta
    curve = grow * grow * rs - 2.0 * grow * alpha * ss + alpha * alpha * st
    alpha2 = new / curve
    c0 = alpha + alpha2 * grow
    c1 = -alpha2 * alpha
    for k in range(3):
        value = total[k] + c0 * total[3 + k] + c1 * total[6 + k]
        for i in range(8):
            points[k : k + 1, i * 128 : i * 128 + 128] = value[i : i + 1]
    slip = points[...] - motion[...]
    speed = jnp.sqrt(jnp.sum(slip * slip, axis=0, keepdims=True) + 1.0)
    force[...] = (-DT * coeff[...] * speed) * slip
    for x in range(X):
        pressure[x] = fields[PRES, x] + c0 * r0[x] + c1 * s[x]
        for k in range(3):
            velocity[k, x] = grads[k, x] + c0 * grads[3 + k, x] + c1 * grads[6 + k, x]
    first = window_start()
    width = 256
    body = jnp.zeros((3 * WINDOW * Y, Z), F32)
    for c in range(host.shape[1] // width):
        cut = slice(c * width, c * width + width)
        z_weights, xy_weights = point_weights(host, off, cut, first)
        scaled = jnp.concatenate(
            [xy_weights[l] * force[k : k + 1, cut] for k in range(3) for l in range(WINDOW)],
            axis=0,
        )
        body = body + lax.dot_general(
            scaled,
            z_weights,
            (((1,), (1,)), ((), ())),
            precision=lax.Precision.HIGHEST,
            preferred_element_type=F32,
        )
    body = body.reshape(3, WINDOW, Y, Z)
    for k in range(3):
        for l in range(WINDOW):
            velocity[k, first + l] = velocity[k, first + l] + body[k, l]


def shift(value, axis, step):
    names = axis if isinstance(axis, tuple) else (axis,)
    n = 1
    for name in names:
        n *= lax.axis_size(name)
    return lax.ppermute(value, axis, [(i, (i + step) % n) for i in range(n)])


def total_over(value, axis, n):
    copies = jnp.broadcast_to(value[None], (n,) + value.shape)
    return jnp.sum(lax.all_to_all(copies, axis, 0, 0), axis=0)


def sds(*shape):
    return jax.ShapeDtypeStruct(shape, F32)


def call(kernel, outs, inputs, scratch=(), name=None, space=None):
    return pl.pallas_call(
        kernel,
        out_shape=outs,
        in_specs=[pl.BlockSpec(memory_space=space or pltpu.VMEM)] * len(inputs),
        out_specs=[VMEM] * len(outs),
        scratch_shapes=scratch,
        compiler_params=PARAMS,
        name=name,
    )(*inputs)


def shards(
    velocity, eddy_visc, solid, pressure_old, relaxation, host_cell, offsets, blade_motion, force_coeff
):
    points = host_cell.shape[1]
    girth = ("gx", "core")
    block, side, unit = sds(X, Y, Z), sds(len(XLAYERS), Y, Z), sds(2, Y, 128)
    fields, up, down, z_up, z_down = call(
        pack_kernel,
        (sds(FIELDS, X, Y, Z), side, side, unit, unit),
        (velocity, eddy_visc, solid, pressure_old, relaxation),
        [pltpu.VMEM((X, Y, Z), jnp.int32), pltpu.SemaphoreType.DMA((5,))],
        name="pack",
        space=pltpu.HBM,
    )
    zm, zp = shift(z_up, "prop", 1), shift(z_down, "prop", -1)
    xm, xp = shift(up, "stream", 1), shift(down, "stream", -1)
    edge = sds(YTILES, 8, Z)
    y_up, y_down = call(edge_kernel, (edge, edge), (fields, zm, zp), name="edges")
    ym, yp = shift(y_up, girth, 1), shift(y_down, girth, -1)
    relay = sds(RTILES, 8, Z)
    ext, r_up, r_down = call(
        block_kernel,
        (sds(FIELDS, X, YE, ZE), relay, relay),
        (fields, zm, zp, ym, yp),
        name="block",
    )
    rm, rp = shift(r_up, "stream", 1), shift(r_down, "stream", -1)
    half = sds(5, 8, 128)
    kept, sent, grads, r0, s = call(
        main_kernel,
        (half, half, sds(9, X, Y, Z), block, block),
        (ext, xm, xp, rm, rp, host_cell, offsets),
        [
            pltpu.VMEM((2, len(XLAYERS), YE, ZE), F32),
            pltpu.VMEM((3, X + 6, YE, ZE), F32),
            pltpu.VMEM((X + 4, YE, ZE), F32),
            pltpu.VMEM((X + 2, YE, ZE), F32),
            pltpu.VMEM((10, 8, 128), F32),
        ],
        name="main",
    )
    mine = kept + shift(sent, "core", 1)
    mine = total_over(mine, ("gx", "prop"), 16)
    mine = total_over(mine, "stream", 8)
    other = shift(mine, "core", 1)
    return call(
        final_kernel,
        (sds(3, X, Y, Z), block, sds(3, points)),
        (
            mine,
            other,
            fields,
            grads,
            r0,
            s,
            host_cell,
            offsets,
            blade_motion,
            force_coeff.reshape(1, points),
        ),
        [pltpu.VMEM((3, points), F32)],
        name="final",
    )


def solution(mesh):
    cut = Mesh(mesh.devices.reshape(8, 4, 2, 4), ("stream", "gx", "core", "prop"))
    cells = ("stream", ("gx", "core"), "prop")
    placed = (P(None, *cells),) + (P(*cells),) * 4 + (P(),) * 4
    return jax.shard_map(
        shards,
        mesh=cut,
        in_specs=placed,
        out_specs=(P(None, *cells), P(*cells), P()),
        check_vma=False,
    )
```

```python
import jax
import jax.numpy as jnp
from jax import lax
from jax.experimental import pallas as pl
from jax.experimental.pallas import tpu as pltpu
from jax.sharding import Mesh, PartitionSpec as P

DT = 0.1
F32 = jnp.float32
BF16 = jnp.bfloat16

X, Y, Z = 8, 16, 256
YE, ZE = 24, 384
VISC, KEEP, PRES, RELAX = 3, 4, 5, 6
FIELDS = 7
RADIUS = (4, 3, 3, 3, 3, 3, 2)
XLAYERS = [(f, d) for f in range(FIELDS) for d in range(1, RADIUS[f] + 1)]
CORNER = (3, 3, 3, 2, 2, 2, 1)
RELAYED = [(f, d) for f in range(FIELDS) for d in range(1, CORNER[f] + 1)]
YPAIRS = FIELDS * X // 2
ZUNITS = -(-FIELDS * X // 32)
RTILES = len(RELAYED) + 2
WINDOW = 3
VMEM = pl.BlockSpec(memory_space=pltpu.VMEM)
MIB = 1024 * 1024


def iota(shape, dim):
    return lax.broadcasted_iota(jnp.int32, shape, dim)


def roll(a, shift, axis):
    shift = shift % a.shape[axis]
    return a if shift == 0 else pltpu.roll(a, shift, axis)


def halves(width=Z):
    return [slice(i, i + 128) for i in range(0, width, 128)]


def load(refs, own_out, stage, sems):
    velocity, visc, solid, pres, relax = refs
    copies = [
        pltpu.make_async_copy(velocity, own_out.at[:3], sems.at[0]),
        pltpu.make_async_copy(visc, own_out.at[VISC], sems.at[1]),
        pltpu.make_async_copy(solid, stage, sems.at[2]),
        pltpu.make_async_copy(pres, own_out.at[PRES], sems.at[3]),
        pltpu.make_async_copy(relax, own_out.at[RELAX], sems.at[4]),
    ]
    for copy in copies:
        copy.start()
    for copy in copies:
        copy.wait()
    own_out[KEEP] = 1.0 - stage[...].astype(F32)


def pack_kernel(*args):
    refs, (fields, y_up, y_down, up, down, stage, sems) = args[:5], args[5:]
    load(refs, fields, stage, sems)
    low_rows = iota((8, Z), 0) < 4
    for t in range(YPAIRS):
        f, x = divmod(2 * t, X)
        a, b = fields[f, x], fields[f, x + 1]
        y_up[t] = jnp.where(low_rows, roll(a[8:], 4, 0), b[8:])
        y_down[t] = jnp.where(low_rows, a[:8], roll(b[:8], 4, 0))
    for i, (f, d) in enumerate(XLAYERS):
        up[i] = fields[f, X - d]
        down[i] = fields[f, d - 1]


def position():
    return (
        lax.axis_index("stream"),
        lax.axis_index("gx") * 2 + lax.axis_index("core"),
        lax.axis_index("prop"),
    )


def inside_flags():
    out = []
    for i, n in zip(position(), (8, 8, 4)):
        out.append((i > 0).astype(F32))
        out.append((i < n - 1).astype(F32))
    return out


def z_pack(tiles, to_up, to_down, slot):
    for unit in range(ZUNITS):
        high = jnp.zeros(slot.shape, F32)
        low = jnp.zeros(slot.shape, F32)
        for j, tile in enumerate(tiles[32 * unit : 32 * unit + 32]):
            high = jnp.where(slot == j, roll(tile[:, Z - 128 :], 4 * j - 124, 1), high)
            low = jnp.where(slot == j, roll(tile[:, :128], 4 * j, 1), low)
        to_up(unit, high)
        to_down(unit, low)


def own_kernel(fields, z_up, z_down):
    tiles = [fields[f, x] for f in range(FIELDS) for x in range(X)]
    z_pack(tiles, z_up.__setitem__, z_down.__setitem__, iota((Y, 128), 1) // 4)


def rows_kernel(own_up, own_down, ym, yp, rows, z_up, z_down):
    _, _, in_ym, in_yp, _, _ = inside_flags()
    low_rows = iota((8, Z), 0) < 4
    for t in range(YPAIRS):
        plus, minus = yp[t] * in_yp, ym[t] * in_ym
        f, x = divmod(2 * t, X)
        rows[f, x] = jnp.where(low_rows, plus, roll(minus, 4, 0))
        rows[f, x + 1] = jnp.where(low_rows, roll(plus, 4, 0), minus)
    for unit in range(ZUNITS):
        z_up[unit, :Y], z_down[unit, :Y] = own_up[unit], own_down[unit]

    def put(out):
        def store(unit, value):
            out[unit, Y:] = value

        return store

    tiles = [rows[f, x] for f in range(FIELDS) for x in range(X)]
    z_pack(tiles, put(z_up), put(z_down), iota((8, 128), 1) // 4)


def third_kernel(rows, zm, zp, third, to_up, to_down):
    in_zm, in_zp = inside_flags()[4:]
    lane = iota((8, 128), 1)
    right = (lane < 4).astype(F32) * in_zp
    left = (lane >= 124).astype(F32) * in_zm
    slot = lane // 8
    for f in range(FIELDS):
        for x in range(X):
            for h in range(3):
                unit, j = divmod(f * X + x, 32)
                cut = slice(8 * h, 8 * h + 8)
                plus, minus = roll(zp[unit, cut], -4 * j, 1), roll(zm[unit, cut], 124 - 4 * j, 1)
                third[f, x, cut] = plus * right + minus * left
    for up, out in ((True, to_up), (False, to_down)):
        units = [jnp.zeros((8, 128), F32) for _ in range(4)]
        for i, (f, d) in enumerate(RELAYED):
            x = X - d if up else d - 1
            out[i] = rows[f, x]
            for h in range(3):
                unit, j = divmod(3 * i + h, 16)
                tile = roll(third[f, x, 8 * h : 8 * h + 8], 8 * j + 4, 1)
                units[unit] = jnp.where(slot == j, tile, units[unit])
        for unit in range(4):
            out[len(RELAYED) + unit // 2, :, halves()[unit % 2]] = units[unit]


def y_plus(a):
    return roll(a, -1, 0)


def y_minus(a):
    return roll(a, 1, 0)


def z_plus(a):
    return roll(a, -1, 1)


def z_minus(a):
    return roll(a, 1, 1)


def own(a):
    return a[:Y, :Z]


def cell_mask():
    _, _, in_ym, in_yp, in_zm, in_zp = inside_flags()
    row, col = iota((YE, ZE), 0), iota((YE, ZE), 1)
    in_y = jnp.where(row < Y, 1.0, jnp.where(row < Y + 4, in_yp, in_ym))
    in_z = jnp.where(
        col < Z, 1.0, jnp.where(col < Z + 4, in_zp, jnp.where(col >= ZE - 4, in_zm, 0.0))
    )
    return in_y * in_z


def beside(get, x):
    center = get(x)
    return [
        (get(x + 1), get(x - 1)),
        (y_plus(center), y_minus(center)),
        (z_plus(center), z_minus(center)),
    ]


def nearby(pairs):
    return sum(p + m for p, m in pairs)


def predicted(field, k, x):
    center = field(k, x)
    pairs = beside(lambda i: field(k, i), x)
    conv = 0.5 * sum(field(d, x) * (p - m) for d, (p, m) in enumerate(pairs))
    lap = nearby(pairs) - 6.0 * center
    return field(KEEP, x) * (center + DT * (field(VISC, x) * lap - conv))


def residual(field, pred, x, mask):
    div = 0.5 * (
        pred(0, x + 1)
        - pred(0, x - 1)
        + (y_plus(pred(1, x)) - y_minus(pred(1, x)))
        + (z_plus(pred(2, x)) - z_minus(pred(2, x)))
    )
    pairs = beside(lambda i: field(PRES, i), x)
    image = (6.0 + field(RELAX, x)) * field(PRES, x) - nearby(pairs)
    return (-div / DT - image) * mask, pairs


def image_of(field, get, x, mask):
    pairs = beside(get, x)
    return ((6.0 + field(RELAX, x)) * get(x) - nearby(pairs)) * mask, pairs


def first_part(field, pred, x, pairs, out, at):
    for d, (p, m) in enumerate(pairs):
        grad = own(p) - own(m)
        out[d, at] = own(field(KEEP, x)) * (own(pred(d, x)) - DT * 0.5 * grad)


def later_part(field, x, pairs, out, start, at):
    keep = own(field(KEEP, x)) * (-DT * 0.5)
    for d, (p, m) in enumerate(pairs):
        out[start + d, at] = keep * (own(p) - own(m))


def extended(fields, rows, third, f, x):
    return jnp.concatenate([jnp.concatenate([fields[f, x], rows[f, x]], axis=0), third[f, x]], axis=1)


def inner_kernel(fields, rows, third, pred_out, res_out, img_out, first_out, second_out):
    def field(f, x):
        return extended(fields, rows, third, f, x)

    def pred(k, x):
        return pred_out[k, x - 1]

    def res(x):
        return res_out[x - 2]

    mask = cell_mask()
    for x in range(1, 7):
        for k in range(3):
            pred_out[k, x - 1] = predicted(field, k, x)
    for x in range(2, 6):
        res_out[x - 2], pairs = residual(field, pred, x, mask)
        first_part(field, pred, x, pairs, first_out, x - 2)
    for x in range(3, 5):
        img_out[x - 3], pairs = image_of(field, res, x, mask)
        later_part(field, x, pairs, second_out, 0, x - 3)


def weight_kernel(host, off, z_high, z_low, xy):
    width = 256
    first = window_start()
    for c in range(host.shape[1] // width):
        cut = slice(c * width, c * width + width)
        place = iota((Z, width), 0) + lax.axis_index("prop") * Z
        weight = axis_weights(host, off, 2, cut, place)
        high = weight.astype(BF16)
        z_high[:, cut] = high
        z_low[:, cut] = (weight - high.astype(F32)).astype(BF16)
        place = iota((Y, width), 0) + position()[1] * Y
        weight = axis_weights(host, off, 1, cut, place)
        x_first = lax.axis_index("stream") * X + first
        for l in range(WINDOW):
            xy[l, :, cut] = weight * axis_weights(host, off, 0, cut, x_first + l)


def product(a, high, low, dims):
    a_high = a.astype(BF16)
    a_low = (a - a_high.astype(F32)).astype(BF16)

    def dot(p, q):
        return lax.dot_general(p, q, (dims, ((), ())), preferred_element_type=F32)

    return dot(a_low, high) + dot(a_high, low) + dot(a_high, high)


def main_kernel(
    fields,
    rows,
    third,
    xm,
    xp,
    rm,
    rp,
    pred_in,
    res_in,
    img_in,
    first_in,
    second_in,
    z_high,
    z_low,
    xy,
    keep_half,
    send_half,
    grads,
    r0_out,
    s_out,
    halo,
    pred_own,
    res_own,
    img_own,
    payload,
):
    in_xm, in_xp = inside_flags()[:2]

    lane = iota((8, 128), 1)
    ends = ((lane < 4) | (lane >= 124)).astype(F32)
    for side, (edge, relay, flag) in enumerate(((xm, rm, in_xm), (xp, rp, in_xp))):
        for i, layer in enumerate(XLAYERS):
            halo[side, i, :Y, :Z] = edge[i] * flag
            if layer not in RELAYED:
                halo[side, i, :Y, Z:] = jnp.zeros((Y, 128), F32)
                halo[side, i, Y:] = jnp.zeros((8, ZE), F32)
                continue
            n = RELAYED.index(layer)
            halo[side, i, Y:, :Z] = relay[n] * flag
            for h in range(3):
                unit, j = divmod(3 * n + h, 16)
                packed = relay[len(RELAYED) + unit // 2, :, halves()[unit % 2]]
                halo[side, i, 8 * h : 8 * h + 8, Z:] = roll(packed, -8 * j - 4, 1) * (ends * flag)

    def field(f, x):
        if x < 0:
            return halo[0, XLAYERS.index((f, -x))]
        if x >= X:
            return halo[1, XLAYERS.index((f, x - X + 1))]
        return extended(fields, rows, third, f, x)

    def pred(k, x):
        return pred_in[k, x - 1] if 1 <= x < 7 else pred_own[k, x + 3]

    def res(x):
        return res_in[x - 2] if 2 <= x < 6 else res_own[x + 2]

    def img(x):
        return img_in[x - 3] if 3 <= x < 5 else img_own[x + 1]

    mask = cell_mask()
    masks = {x: mask * in_xm for x in (-2, -1)}
    masks.update({x: mask * in_xp for x in (X, X + 1)})
    for x in (-3, -2, -1, 0, 7, 8, 9, 10):
        for k in range(3 if -3 < x < X + 2 else 1):
            pred_own[k, x + 3] = predicted(field, k, x)
    for x in range(-2, X + 2):
        if not 2 <= x < 6:
            res_own[x + 2], pairs = residual(field, pred, x, masks.get(x, mask))
            if 0 <= x < X:
                first_part(field, pred, x, pairs, grads, x)
    grads[:3, 2:6] = first_in[...]
    for x in range(-1, X + 1):
        if not 3 <= x < 5:
            img_own[x + 1], pairs = image_of(field, res, x, masks.get(x, mask))
            if 0 <= x < X:
                later_part(field, x, pairs, grads, 3, x)
    grads[3:6, 3:5] = second_in[...]
    sums = [jnp.zeros((Y, Z), F32) for _ in range(4)]
    for x in range(X):
        image, pairs = image_of(field, img, x, 1.0)
        later_part(field, x, pairs, grads, 6, x)
        r, s = own(res(x)), own(img(x))
        r0_out[x], s_out[x] = r, s
        for i, (a, b) in enumerate(((r, r), (r, s), (s, s), (s, own(image)))):
            sums[i] = sums[i] + a * b
    payload[9] = jnp.zeros((8, 128), F32)
    for i, total in enumerate(sums):
        line = jnp.sum(total[:, :128] + total[:, 128:], axis=0, keepdims=True)
        payload[9, i : i + 1] = line

    samples = grads[:, pl.ds(window_start(), WINDOW)].reshape(9 * WINDOW * Y, Z)
    width = 256
    for c in range(z_high.shape[1] // width):
        cut = slice(c * width, c * width + width)
        parts = product(samples, z_high[:, cut], z_low[:, cut], ((1,), (0,)))
        parts = parts.reshape(9, WINDOW, Y, width)
        for k in range(9):
            total = sum(parts[k, l] * xy[l, :, cut] for l in range(WINDOW))
            line = jnp.sum(total, axis=0, keepdims=True)
            for half, piece in enumerate(halves(width)):
                at = c * (width // 128) + half
                payload[k, at : at + 1] = line[:, piece]
    second = lax.axis_index("core") == 1
    for k in range(5):
        keep_half[k] = jnp.where(second, payload[5 + k], payload[k])
        send_half[k] = jnp.where(second, payload[k], payload[5 + k])


def window_start():
    return jnp.where(lax.axis_index("stream") * X + X == 32, X - WINDOW, 0)


def axis_weights(host, off, d, cut, place):
    low = host[d : d + 1, cut]
    part = off[d : d + 1, cut]
    return jnp.where(place == low, 1.0 - part, 0.0) + jnp.where(place == low + 1, part, 0.0)


def final_kernel(
    mine,
    other,
    pres,
    grads,
    r0,
    s,
    z_high,
    z_low,
    xy,
    motion,
    coeff,
    velocity,
    pressure,
    points,
    force,
):
    second = lax.axis_index("core") == 1
    total = [jnp.where(second, other[k], mine[k]) for k in range(5)]
    total += [jnp.where(second, mine[k], other[k]) for k in range(5)]
    lines = total[9]
    rr, rs, ss, st = [jnp.sum(lines[i : i + 1], axis=1, keepdims=True) for i in range(4)]
    alpha = rr / rs
    new = rr - 2.0 * alpha * rs + alpha * alpha * ss
    beta = new / rr
    grow = 1.0 + beta
    curve = grow * grow * rs - 2.0 * grow * alpha * ss + alpha * alpha * st
    alpha2 = new / curve
    c0 = alpha + alpha2 * grow
    c1 = -alpha2 * alpha
    for k in range(3):
        value = total[k] + c0 * total[3 + k] + c1 * total[6 + k]
        for i in range(8):
            points[k : k + 1, i * 128 : i * 128 + 128] = value[i : i + 1]
    slip = points[...] - motion[...]
    speed = jnp.sqrt(jnp.sum(slip * slip, axis=0, keepdims=True) + 1.0)
    force[...] = (-DT * coeff[...] * speed) * slip
    for x in range(X):
        pressure[x] = pres[x] + c0 * r0[x] + c1 * s[x]
        for k in range(3):
            velocity[k, x] = grads[k, x] + c0 * grads[3 + k, x] + c1 * grads[6 + k, x]
    first = window_start()
    width = 256
    body = jnp.zeros((3 * WINDOW * Y, Z), F32)
    for c in range(z_high.shape[1] // width):
        cut = slice(c * width, c * width + width)
        scaled = jnp.concatenate(
            [xy[l, :, cut] * force[k : k + 1, cut] for k in range(3) for l in range(WINDOW)],
            axis=0,
        )
        body = body + product(scaled, z_high[:, cut], z_low[:, cut], ((1,), (1,)))
    body = body.reshape(3, WINDOW, Y, Z)
    for k in range(3):
        for l in range(WINDOW):
            velocity[k, first + l] = velocity[k, first + l] + body[k, l]


def shift(value, axis, step):
    names = axis if isinstance(axis, tuple) else (axis,)
    n = 1
    for name in names:
        n *= lax.axis_size(name)
    return lax.ppermute(value, axis, [(i, (i + step) % n) for i in range(n)])


def total_over(value, axis, n):
    copies = jnp.broadcast_to(value[None], (n,) + value.shape)
    return jnp.sum(lax.all_to_all(copies, axis, 0, 0), axis=0)


def sds(*shape, dtype=F32):
    return jax.ShapeDtypeStruct(shape, dtype)


def call(kernel, outs, inputs, scratch=(), name=None, space=None, limit=16, us=1.0):
    return pl.pallas_call(
        kernel,
        out_shape=outs,
        in_specs=[pl.BlockSpec(memory_space=space or pltpu.VMEM)] * len(inputs),
        out_specs=[VMEM] * len(outs),
        scratch_shapes=scratch,
        compiler_params=pltpu.CompilerParams(vmem_limit_bytes=limit * MIB),
        cost_estimate=pl.CostEstimate(
            flops=0, bytes_accessed=int(us * 3.0e6), transcendentals=0
        ),
        name=name,
    )(*inputs)


def shards(
    velocity, eddy_visc, solid, pressure_old, relaxation, host_cell, offsets, blade_motion, force_coeff
):
    points = host_cell.shape[1]
    girth = ("gx", "core")
    block, side, edge = sds(X, Y, Z), sds(len(XLAYERS), Y, Z), sds(YPAIRS, 8, Z)
    fields, y_up, y_down, up, down = call(
        pack_kernel,
        (sds(FIELDS, X, Y, Z), edge, edge, side, side),
        (velocity, eddy_visc, solid, pressure_old, relaxation),
        [pltpu.VMEM((X, Y, Z), jnp.int32), pltpu.SemaphoreType.DMA((5,))],
        name="pack",
        space=pltpu.HBM,
        limit=56,
    )
    ym, yp = shift(y_up, girth, 1), shift(y_down, girth, -1)
    xm, xp = shift(up, "stream", 1), shift(down, "stream", -1)
    unit, own_unit = sds(ZUNITS, YE, 128), sds(ZUNITS, Y, 128)
    own_up, own_down = call(own_kernel, (own_unit, own_unit), (fields,), name="ownz", us=0.5)
    rows, z_up, z_down = call(
        rows_kernel, (sds(FIELDS, X, 8, Z), unit, unit), (own_up, own_down, ym, yp), name="rows", us=0.1
    )
    zm, zp = shift(z_up, "prop", 1), shift(z_down, "prop", -1)
    relay = sds(RTILES, 8, Z)
    third, r_up, r_down = call(
        third_kernel,
        (sds(FIELDS, X, YE, 128), relay, relay),
        (rows, zm, zp),
        name="third",
        us=0.1,
    )
    wide = sds(Z, points, dtype=BF16)
    weights = call(
        weight_kernel, (wide, wide, sds(WINDOW, Y, points)), (host_cell, offsets), name="weights", us=0.5
    )
    inner = call(
        inner_kernel,
        (
            sds(3, 6, YE, ZE),
            sds(4, YE, ZE),
            sds(2, YE, ZE),
            sds(3, 4, Y, Z),
            sds(3, 2, Y, Z),
        ),
        (fields, rows, third),
        name="inner",
        us=1.5,
    )
    rm, rp = shift(r_up, "stream", 1), shift(r_down, "stream", -1)
    half = sds(5, 8, 128)
    kept, sent, grads, r0, s = call(
        main_kernel,
        (half, half, sds(9, X, Y, Z), block, block),
        (fields, rows, third, xm, xp, rm, rp, *inner, *weights),
        [
            pltpu.VMEM((2, len(XLAYERS), YE, ZE), F32),
            pltpu.VMEM((3, X + 6, YE, ZE), F32),
            pltpu.VMEM((X + 4, YE, ZE), F32),
            pltpu.VMEM((X + 2, YE, ZE), F32),
            pltpu.VMEM((10, 8, 128), F32),
        ],
        name="main",
    )
    mine = kept + shift(sent, "core", 1)
    mine = total_over(mine, ("gx", "prop"), 16)
    mine = total_over(mine, "stream", 8)
    other = shift(mine, "core", 1)
    return call(
        final_kernel,
        (sds(3, X, Y, Z), block, sds(3, points)),
        (
            mine,
            other,
            pressure_old,
            grads,
            r0,
            s,
            *weights,
            blade_motion,
            force_coeff.reshape(1, points),
        ),
        [pltpu.VMEM((3, points), F32)],
        name="final",
    )


def solution(mesh):
    cut = Mesh(mesh.devices.reshape(8, 4, 2, 4), ("stream", "gx", "core", "prop"))
    cells = ("stream", ("gx", "core"), "prop")
    placed = (P(None, *cells),) + (P(*cells),) * 4 + (P(),) * 4
    return jax.shard_map(
        shards,
        mesh=cut,
        in_specs=placed,
        out_specs=(P(None, *cells), P(*cells), P()),
        check_vma=False,
    )
```

```python
import jax
import jax.numpy as jnp
from jax import lax
from jax.experimental import pallas as pl
from jax.experimental.pallas import tpu as pltpu
from jax.sharding import Mesh, PartitionSpec as P

DT = 0.1
F32 = jnp.float32
BF16 = jnp.bfloat16

X, Y, Z = 8, 16, 256
YE, ZE = 24, 384
VISC, KEEP, PRES, RELAX = 3, 4, 5, 6
FIELDS = 7
RADIUS = (4, 3, 3, 3, 3, 3, 2)
XLAYERS = [(f, d) for f in range(FIELDS) for d in range(1, RADIUS[f] + 1)]
CORNER = (3, 3, 3, 2, 2, 2, 1)
RELAYED = [(f, d) for f in range(FIELDS) for d in range(1, CORNER[f] + 1)]
SHARED = [(f, d) for f, d in RELAYED if d < CORNER[f]]
YPAIRS = FIELDS * X // 2
ZUNITS = -(-FIELDS * X // 32)
SHARED += [(f, d) for f, d in RELAYED if CORNER[f] == 1]
RTILES = len(SHARED) + 2
WINDOW = 3
VMEM = pl.BlockSpec(memory_space=pltpu.VMEM)
MIB = 1024 * 1024


def iota(shape, dim):
    return lax.broadcasted_iota(jnp.int32, shape, dim)


def roll(a, shift, axis):
    shift = shift % a.shape[axis]
    return a if shift == 0 else pltpu.roll(a, shift, axis)


def halves(width=Z):
    return [slice(i, i + 128) for i in range(0, width, 128)]


def load(refs, own_out, stage, sems):
    velocity, visc, solid, pres, relax = refs
    copies = [
        pltpu.make_async_copy(velocity, own_out.at[:3], sems.at[0]),
        pltpu.make_async_copy(visc, own_out.at[VISC], sems.at[1]),
        pltpu.make_async_copy(solid, stage, sems.at[2]),
        pltpu.make_async_copy(pres, own_out.at[PRES], sems.at[3]),
        pltpu.make_async_copy(relax, own_out.at[RELAX], sems.at[4]),
    ]
    for copy in copies:
        copy.start()
    for copy in copies:
        copy.wait()
    own_out[KEEP] = 1.0 - stage[...].astype(F32)


def pack_kernel(*args):
    refs, (fields, y_up, y_down, up, down, stage, sems) = args[:5], args[5:]
    load(refs, fields, stage, sems)
    low_rows = iota((8, Z), 0) < 4
    for t in range(YPAIRS):
        f, x = divmod(2 * t, X)
        a, b = fields[f, x], fields[f, x + 1]
        y_up[t] = jnp.where(low_rows, roll(a[8:], 4, 0), b[8:])
        y_down[t] = jnp.where(low_rows, a[:8], roll(b[:8], 4, 0))
    for i, (f, d) in enumerate(XLAYERS):
        up[i], down[i] = fields[f, X - d], fields[f, d - 1]


def position():
    return (
        lax.axis_index("stream"),
        lax.axis_index("gx") * 2 + lax.axis_index("core"),
        lax.axis_index("prop"),
    )


def inside_flags():
    out = []
    for i, n in zip(position(), (8, 8, 4)):
        out.append((i > 0).astype(F32))
        out.append((i < n - 1).astype(F32))
    return out


def z_pack(tiles, to_up, to_down, slot):
    for unit in range(ZUNITS):
        high = jnp.zeros(slot.shape, F32)
        low = jnp.zeros(slot.shape, F32)
        for j, tile in enumerate(tiles[32 * unit : 32 * unit + 32]):
            high = jnp.where(slot == j, roll(tile[:, Z - 128 :], 4 * j - 124, 1), high)
            low = jnp.where(slot == j, roll(tile[:, :128], 4 * j, 1), low)
        to_up(unit, high)
        to_down(unit, low)


def own_kernel(fields, z_up, z_down):
    tiles = [fields[f, x] for f in range(FIELDS) for x in range(X)]
    z_pack(tiles, z_up.__setitem__, z_down.__setitem__, iota((Y, 128), 1) // 4)


def rows_kernel(own_up, own_down, ym, yp, rows, z_up, z_down):
    _, _, in_ym, in_yp, _, _ = inside_flags()
    low_rows = iota((8, Z), 0) < 4
    for t in range(YPAIRS):
        minus, plus = ym[t], yp[t]
        plus, minus = plus * in_yp, minus * in_ym
        f, x = divmod(2 * t, X)
        rows[f, x] = jnp.where(low_rows, plus, roll(minus, 4, 0))
        rows[f, x + 1] = jnp.where(low_rows, roll(plus, 4, 0), minus)
    tiles = [rows[f, x] for f in range(FIELDS) for x in range(X)]
    ups, downs = {}, {}
    z_pack(tiles, ups.__setitem__, downs.__setitem__, iota((8, 128), 1) // 4)
    for unit in range(ZUNITS):
        z_up[unit, :Y], z_down[unit, :Y] = own_up[unit], own_down[unit]
        z_up[unit, Y:], z_down[unit, Y:] = ups[unit], downs[unit]


def third_kernel(rows, zm, zp, third, r_up, r_down):
    in_zm, in_zp = inside_flags()[4:]
    lane = iota((8, 128), 1)
    right = (lane < 4).astype(F32) * in_zp
    left = (lane >= 124).astype(F32) * in_zm
    slot = lane // 8
    row = iota((8, Z), 0)
    outer_rows = (row < 2) | (row >= 6)
    for f in range(FIELDS):
        for x in range(X):
            for h in range(3):
                unit, j = divmod(f * X + x, 32)
                cut = slice(8 * h, 8 * h + 8)
                plus, minus = roll(zp[unit, cut], -4 * j, 1), roll(zm[unit, cut], 124 - 4 * j, 1)
                third[f, x, cut] = plus * right + minus * left
    to_up, to_down = {}, {}
    for up, out in ((True, to_up), (False, to_down)):
        units = [jnp.zeros((8, 128), F32) for _ in range(4)]
        for i, (f, d) in enumerate(RELAYED):
            x = X - d if up else d - 1
            if (f, d) in SHARED:
                tile = rows[f, x]
                if d + 1 == CORNER[f]:
                    after = rows[f, x - 1 if up else x + 1]
                    tile = jnp.where(outer_rows, tile, roll(after, 4, 0))
                out[SHARED.index((f, d))] = tile
            for h in range(3):
                unit, j = divmod(3 * i + h, 16)
                tile = roll(third[f, x, 8 * h : 8 * h + 8], 8 * j + 4, 1)
                units[unit] = jnp.where(slot == j, tile, units[unit])
        for unit in range(0, 4, 2):
            out[len(SHARED) + unit // 2] = jnp.concatenate(units[unit : unit + 2], axis=1)
    for t in range(RTILES):
        r_up[t], r_down[t] = to_up[t], to_down[t]


def y_plus(a):
    return roll(a, -1, 0)


def y_minus(a):
    return roll(a, 1, 0)


def z_plus(a):
    return roll(a, -1, 1)


def z_minus(a):
    return roll(a, 1, 1)


def own(a):
    return a[:Y, :Z]


def cell_mask():
    _, _, in_ym, in_yp, in_zm, in_zp = inside_flags()
    row, col = iota((YE, ZE), 0), iota((YE, ZE), 1)
    in_y = jnp.where(row < Y, 1.0, jnp.where(row < Y + 4, in_yp, in_ym))
    in_z = jnp.where(
        col < Z, 1.0, jnp.where(col < Z + 4, in_zp, jnp.where(col >= ZE - 4, in_zm, 0.0))
    )
    return in_y * in_z


def beside(get, x):
    center = get(x)
    return [
        (get(x + 1), get(x - 1)),
        (y_plus(center), y_minus(center)),
        (z_plus(center), z_minus(center)),
    ]


def nearby(pairs):
    return sum(p + m for p, m in pairs)


def predicted(field, k, x):
    center = field(k, x)
    pairs = beside(lambda i: field(k, i), x)
    conv = 0.5 * sum(field(d, x) * (p - m) for d, (p, m) in enumerate(pairs))
    lap = nearby(pairs) - 6.0 * center
    return field(KEEP, x) * (center + DT * (field(VISC, x) * lap - conv))


def residual(field, pred, x, mask):
    div = 0.5 * (
        pred(0, x + 1)
        - pred(0, x - 1)
        + (y_plus(pred(1, x)) - y_minus(pred(1, x)))
        + (z_plus(pred(2, x)) - z_minus(pred(2, x)))
    )
    pairs = beside(lambda i: field(PRES, i), x)
    image = (6.0 + field(RELAX, x)) * field(PRES, x) - nearby(pairs)
    return (-div / DT - image) * mask, pairs


def image_of(field, get, x, mask):
    pairs = beside(get, x)
    return ((6.0 + field(RELAX, x)) * get(x) - nearby(pairs)) * mask, pairs


def first_part(field, pred, x, pairs, out, at):
    for d, (p, m) in enumerate(pairs):
        grad = own(p) - own(m)
        out[d, at] = own(field(KEEP, x)) * (own(pred(d, x)) - DT * 0.5 * grad)


def later_part(field, x, pairs, out, start, at):
    keep = own(field(KEEP, x)) * (-DT * 0.5)
    for d, (p, m) in enumerate(pairs):
        out[start + d, at] = keep * (own(p) - own(m))


def extended(fields, rows, third, f, x):
    return jnp.concatenate([jnp.concatenate([fields[f, x], rows[f, x]], axis=0), third[f, x]], axis=1)


def inner_kernel(fields, rows, third, pred_out, res_out, img_out, first_out, second_out):
    def field(f, x):
        return extended(fields, rows, third, f, x)

    def pred(k, x):
        return pred_out[k, x - 1]

    def res(x):
        return res_out[x - 2]

    mask = cell_mask()
    for x in range(1, 7):
        for k in range(3):
            pred_out[k, x - 1] = predicted(field, k, x)
    for x in range(2, 6):
        res_out[x - 2], pairs = residual(field, pred, x, mask)
        first_part(field, pred, x, pairs, first_out, x - 2)
    for x in range(3, 5):
        img_out[x - 3], pairs = image_of(field, res, x, mask)
        later_part(field, x, pairs, second_out, 0, x - 3)


def weight_kernel(host, off, z_high, z_low, xy):
    width = 256
    first = window_start()
    for c in range(host.shape[1] // width):
        cut = slice(c * width, c * width + width)
        place = iota((Z, width), 0) + lax.axis_index("prop") * Z
        weight = axis_weights(host, off, 2, cut, place)
        high = weight.astype(BF16)
        z_high[:, cut] = high
        z_low[:, cut] = (weight - high.astype(F32)).astype(BF16)
        place = iota((Y, width), 0) + position()[1] * Y
        weight = axis_weights(host, off, 1, cut, place)
        x_first = lax.axis_index("stream") * X + first
        for l in range(WINDOW):
            xy[l, :, cut] = weight * axis_weights(host, off, 0, cut, x_first + l)


def product(a, high, low, dims):
    a_high = a.astype(BF16)
    a_low = (a - a_high.astype(F32)).astype(BF16)

    def dot(p, q):
        return lax.dot_general(p, q, (dims, ((), ())), preferred_element_type=F32)

    return dot(a_low, high) + dot(a_high, low) + dot(a_high, high)


def main_kernel(
    fields,
    rows,
    third,
    xm,
    xp,
    rm,
    rp,
    pred_in,
    res_in,
    img_in,
    first_in,
    second_in,
    z_high,
    z_low,
    xy,
    keep_half,
    send_half,
    grads,
    r0_out,
    s_out,
    halo,
    pred_own,
    res_own,
    img_own,
    payload,
):
    in_xm, in_xp = inside_flags()[:2]

    lane = iota((8, 128), 1)
    ends = ((lane < 4) | (lane >= 124)).astype(F32)
    for side, (edge, relay, flag) in enumerate(((xm, rm, in_xm), (xp, rp, in_xp))):
        for i, layer in enumerate(XLAYERS):
            halo[side, i, :Y, :Z] = edge[i] * flag
            if layer not in RELAYED:
                halo[side, i, :Y, Z:] = jnp.zeros((Y, 128), F32)
                halo[side, i, Y:] = jnp.zeros((8, ZE), F32)
                continue
            n = RELAYED.index(layer)
            if layer in SHARED:
                tile = relay[SHARED.index(layer)]
            else:
                tile = roll(relay[SHARED.index((layer[0], layer[1] - 1))], 4, 0)
            halo[side, i, Y:, :Z] = tile * flag
            for h in range(3):
                unit, j = divmod(3 * n + h, 16)
                packed = relay[len(SHARED) + unit // 2, :, halves()[unit % 2]]
                halo[side, i, 8 * h : 8 * h + 8, Z:] = roll(packed, -8 * j - 4, 1) * (ends * flag)

    def field(f, x):
        if x < 0:
            return halo[0, XLAYERS.index((f, -x))]
        if x >= X:
            return halo[1, XLAYERS.index((f, x - X + 1))]
        return extended(fields, rows, third, f, x)

    def pred(k, x):
        return pred_in[k, x - 1] if 1 <= x < 7 else pred_own[k, x + 3]

    def res(x):
        return res_in[x - 2] if 2 <= x < 6 else res_own[x + 2]

    def img(x):
        return img_in[x - 3] if 3 <= x < 5 else img_own[x + 1]

    mask = cell_mask()
    masks = {x: mask * in_xm for x in (-2, -1)}
    masks.update({x: mask * in_xp for x in (X, X + 1)})
    for x in (-3, -2, -1, 0, 7, 8, 9, 10):
        for k in range(3 if -3 < x < X + 2 else 1):
            pred_own[k, x + 3] = predicted(field, k, x)
    for x in range(-2, X + 2):
        if not 2 <= x < 6:
            res_own[x + 2], pairs = residual(field, pred, x, masks.get(x, mask))
            if 0 <= x < X:
                first_part(field, pred, x, pairs, grads, x)
    grads[:3, 2:6] = first_in[...]
    for x in range(-1, X + 1):
        if not 3 <= x < 5:
            img_own[x + 1], pairs = image_of(field, res, x, masks.get(x, mask))
            if 0 <= x < X:
                later_part(field, x, pairs, grads, 3, x)
    grads[3:6, 3:5] = second_in[...]
    sums = [jnp.zeros((Y, Z), F32) for _ in range(4)]
    for x in range(X):
        image, pairs = image_of(field, img, x, 1.0)
        later_part(field, x, pairs, grads, 6, x)
        r, s = own(res(x)), own(img(x))
        r0_out[x], s_out[x] = r, s
        for i, (a, b) in enumerate(((r, r), (r, s), (s, s), (s, own(image)))):
            sums[i] = sums[i] + a * b
    payload[9] = jnp.zeros((8, 128), F32)
    for i, total in enumerate(sums):
        line = jnp.sum(total[:, :128] + total[:, 128:], axis=0, keepdims=True)
        payload[9, i : i + 1] = line

    samples = grads[:, pl.ds(window_start(), WINDOW)].reshape(9 * WINDOW * Y, Z)
    width = 256
    for c in range(z_high.shape[1] // width):
        cut = slice(c * width, c * width + width)
        parts = product(samples, z_high[:, cut], z_low[:, cut], ((1,), (0,)))
        parts = parts.reshape(9, WINDOW, Y, width)
        for k in range(9):
            total = sum(parts[k, l] * xy[l, :, cut] for l in range(WINDOW))
            line = jnp.sum(total, axis=0, keepdims=True)
            for half, piece in enumerate(halves(width)):
                at = c * (width // 128) + half
                payload[k, at : at + 1] = line[:, piece]
    second = lax.axis_index("core") == 1
    for k in range(5):
        keep_half[k] = jnp.where(second, payload[5 + k], payload[k])
        send_half[k] = jnp.where(second, payload[k], payload[5 + k])


def window_start():
    return jnp.where(lax.axis_index("stream") * X + X == 32, X - WINDOW, 0)


def axis_weights(host, off, d, cut, place):
    low = host[d : d + 1, cut]
    part = off[d : d + 1, cut]
    return jnp.where(place == low, 1.0 - part, 0.0) + jnp.where(place == low + 1, part, 0.0)


def final_kernel(
    mine,
    other,
    pres,
    grads,
    r0,
    s,
    z_high,
    z_low,
    xy,
    motion,
    coeff,
    velocity,
    pressure,
    points,
    force,
):
    second = lax.axis_index("core") == 1
    total = [jnp.where(second, other[k], mine[k]) for k in range(5)]
    total += [jnp.where(second, mine[k], other[k]) for k in range(5)]
    lines = total[9]
    rr, rs, ss, st = [jnp.sum(lines[i : i + 1], axis=1, keepdims=True) for i in range(4)]
    alpha = rr / rs
    new = rr - 2.0 * alpha * rs + alpha * alpha * ss
    beta = new / rr
    grow = 1.0 + beta
    curve = grow * grow * rs - 2.0 * grow * alpha * ss + alpha * alpha * st
    alpha2 = new / curve
    c0 = alpha + alpha2 * grow
    c1 = -alpha2 * alpha
    for k in range(3):
        value = total[k] + c0 * total[3 + k] + c1 * total[6 + k]
        for i in range(8):
            points[k : k + 1, i * 128 : i * 128 + 128] = value[i : i + 1]
    slip = points[...] - motion[...]
    speed = jnp.sqrt(jnp.sum(slip * slip, axis=0, keepdims=True) + 1.0)
    force[...] = (-DT * coeff[...] * speed) * slip
    for x in range(X):
        pressure[x] = pres[x] + c0 * r0[x] + c1 * s[x]
        for k in range(3):
            velocity[k, x] = grads[k, x] + c0 * grads[3 + k, x] + c1 * grads[6 + k, x]
    first = window_start()
    width = 256
    body = jnp.zeros((3 * WINDOW * Y, Z), F32)
    for c in range(z_high.shape[1] // width):
        cut = slice(c * width, c * width + width)
        scaled = jnp.concatenate(
            [xy[l, :, cut] * force[k : k + 1, cut] for k in range(3) for l in range(WINDOW)],
            axis=0,
        )
        body = body + product(scaled, z_high[:, cut], z_low[:, cut], ((1,), (1,)))
    body = body.reshape(3, WINDOW, Y, Z)
    for k in range(3):
        for l in range(WINDOW):
            velocity[k, first + l] = velocity[k, first + l] + body[k, l]


def exchange(up, down, axis, n):
    before = lax.ppermute(up, axis, [(i, (i + 1) % n) for i in range(n)])
    after = lax.ppermute(down, axis, [(i, (i - 1) % n) for i in range(n)])
    return before, after


def swap_cores(value):
    return lax.ppermute(value, "core", [(0, 1), (1, 0)])


def total_over(value, axis, n):
    copies = jnp.broadcast_to(value[None], (n,) + value.shape)
    return jnp.sum(lax.all_to_all(copies, axis, 0, 0), axis=0)


def sds(*shape, dtype=F32):
    return jax.ShapeDtypeStruct(shape, dtype)


def call(kernel, outs, inputs, scratch=(), name=None, space=None, limit=16, us=1.0):
    return pl.pallas_call(
        kernel,
        out_shape=outs,
        in_specs=[pl.BlockSpec(memory_space=space or pltpu.VMEM)] * len(inputs),
        out_specs=[VMEM] * len(outs),
        scratch_shapes=scratch,
        compiler_params=pltpu.CompilerParams(vmem_limit_bytes=limit * MIB),
        cost_estimate=pl.CostEstimate(
            flops=0, bytes_accessed=int(us * 3.0e6), transcendentals=0
        ),
        name=name,
    )(*inputs)


def shards(
    velocity, eddy_visc, solid, pressure_old, relaxation, host_cell, offsets, blade_motion, force_coeff
):
    points = host_cell.shape[1]
    girth = ("gx", "core")
    block, side, edge = sds(X, Y, Z), sds(len(XLAYERS), Y, Z), sds(YPAIRS, 8, Z)
    fields, y_up, y_down, x_up, x_down = call(
        pack_kernel,
        (sds(FIELDS, X, Y, Z), edge, edge, side, side),
        [
            pltpu.with_memory_space_constraint(a, pltpu.HBM)
            for a in (velocity, eddy_visc, solid, pressure_old, relaxation)
        ],
        [pltpu.VMEM((X, Y, Z), jnp.int32), pltpu.SemaphoreType.DMA((5,))],
        name="pack",
        space=pltpu.HBM,
        limit=24,
    )
    from_y = exchange(y_up, y_down, girth, 8)
    from_x = exchange(x_up, x_down, "stream", 8)
    unit, own_unit = sds(ZUNITS, YE, 128), sds(ZUNITS, Y, 128)
    own_up, own_down = call(own_kernel, (own_unit, own_unit), (fields,), name="ownz", us=0.5)
    rows, z_up, z_down = call(
        rows_kernel, (sds(FIELDS, X, 8, Z), unit, unit), (own_up, own_down, *from_y), name="rows", us=0.1
    )
    from_z = exchange(z_up, z_down, "prop", 4)
    relay = sds(RTILES, 8, Z)
    third, r_up, r_down = call(
        third_kernel,
        (sds(FIELDS, X, YE, 128), relay, relay),
        (rows, *from_z),
        name="third",
        us=0.1,
    )
    wide = sds(Z, points, dtype=BF16)
    weights = call(
        weight_kernel, (wide, wide, sds(WINDOW, Y, points)), (host_cell, offsets), name="weights", us=0.5
    )
    inner = call(
        inner_kernel,
        (
            sds(3, 6, YE, ZE),
            sds(4, YE, ZE),
            sds(2, YE, ZE),
            sds(3, 4, Y, Z),
            sds(3, 2, Y, Z),
        ),
        (fields, rows, third),
        name="inner",
        us=1.5,
    )
    from_r = exchange(r_up, r_down, "stream", 8)
    half = sds(5, 8, 128)
    kept, sent, grads, r0, s = call(
        main_kernel,
        (half, half, sds(9, X, Y, Z), block, block),
        (fields, rows, third, *from_x, *from_r, *inner, *weights),
        [
            pltpu.VMEM((2, len(XLAYERS), YE, ZE), F32),
            pltpu.VMEM((3, X + 6, YE, ZE), F32),
            pltpu.VMEM((X + 4, YE, ZE), F32),
            pltpu.VMEM((X + 2, YE, ZE), F32),
            pltpu.VMEM((10, 8, 128), F32),
        ],
        name="main",
    )
    mine = kept + swap_cores(sent)
    mine = total_over(mine, ("gx", "prop"), 16)
    mine = total_over(mine, "stream", 8)
    other = swap_cores(mine)
    return call(
        final_kernel,
        (sds(3, X, Y, Z), block, sds(3, points)),
        (
            mine,
            other,
            pressure_old,
            grads,
            r0,
            s,
            *weights,
            blade_motion,
            force_coeff.reshape(1, points),
        ),
        [pltpu.VMEM((3, points), F32)],
        name="final",
    )


def solution(mesh):
    cut = Mesh(mesh.devices.reshape(8, 4, 2, 4), ("stream", "gx", "core", "prop"))
    cells = ("stream", ("gx", "core"), "prop")
    placed = (P(None, *cells),) + (P(*cells),) * 4 + (P(),) * 4
    return jax.shard_map(
        shards,
        mesh=cut,
        in_specs=placed,
        out_specs=(P(None, *cells), P(*cells), P()),
        check_vma=False,
    )
```

```python
import jax
import jax.numpy as jnp
from jax import lax
from jax.experimental import pallas as pl
from jax.experimental.pallas import tpu as pltpu
from jax.sharding import Mesh, PartitionSpec as P

DT = 0.1
F32 = jnp.float32
BF16 = jnp.bfloat16

X, Y, Z = 8, 16, 256
YE, ZE = 24, 384
VISC, KEEP, PRES, RELAX = 3, 4, 5, 6
FIELDS = 7
RADIUS = (4, 3, 3, 3, 3, 3, 2)
XLAYERS = [(f, d) for f in range(FIELDS) for d in range(1, RADIUS[f] + 1)]
CORNER = (3, 3, 3, 2, 2, 2, 1)
RELAYED = [(f, d) for f in range(FIELDS) for d in range(1, CORNER[f] + 1)]
SHARED = [(f, d) for f, d in RELAYED if d < CORNER[f]]
YPAIRS = FIELDS * X // 2
ZUNITS = -(-FIELDS * X // 32)
SHARED += [(f, d) for f, d in RELAYED if CORNER[f] == 1]
RTILES = len(SHARED) + 2
WINDOW = 3
VMEM = pl.BlockSpec(memory_space=pltpu.VMEM)
MIB = 1024 * 1024


def iota(shape, dim):
    return lax.broadcasted_iota(jnp.int32, shape, dim)


def roll(a, shift, axis):
    shift = shift % a.shape[axis]
    return a if shift == 0 else pltpu.roll(a, shift, axis)


def halves(width=Z):
    return [slice(i, i + 128) for i in range(0, width, 128)]


def load(refs, own_out, stage, sems):
    velocity, visc, solid, pres, relax = refs
    copies = [
        pltpu.make_async_copy(velocity, own_out.at[:3], sems.at[0]),
        pltpu.make_async_copy(visc, own_out.at[VISC], sems.at[1]),
        pltpu.make_async_copy(solid, stage, sems.at[2]),
        pltpu.make_async_copy(pres, own_out.at[PRES], sems.at[3]),
        pltpu.make_async_copy(relax, own_out.at[RELAX], sems.at[4]),
    ]
    for copy in copies:
        copy.start()
    for copy in copies:
        copy.wait()
    own_out[KEEP] = 1.0 - stage[...].astype(F32)


def pack_kernel(*args):
    refs, (fields, y_up, y_down, up, down, stage, sems) = args[:5], args[5:]
    load(refs, fields, stage, sems)
    low_rows = iota((8, Z), 0) < 4
    for t in range(YPAIRS):
        f, x = divmod(2 * t, X)
        a, b = fields[f, x], fields[f, x + 1]
        y_up[t] = jnp.where(low_rows, roll(a[8:], 4, 0), b[8:])
        y_down[t] = jnp.where(low_rows, a[:8], roll(b[:8], 4, 0))
    for i, (f, d) in enumerate(XLAYERS):
        up[i], down[i] = fields[f, X - d], fields[f, d - 1]


def position():
    return (
        lax.axis_index("stream"),
        lax.axis_index("gx") * 2 + lax.axis_index("core"),
        lax.axis_index("prop"),
    )


def inside_flags():
    out = []
    for i, n in zip(position(), (8, 8, 4)):
        out.append((i > 0).astype(F32))
        out.append((i < n - 1).astype(F32))
    return out


def z_pack(tiles, to_up, to_down, slot):
    for unit in range(ZUNITS):
        high = jnp.zeros(slot.shape, F32)
        low = jnp.zeros(slot.shape, F32)
        for j, tile in enumerate(tiles[32 * unit : 32 * unit + 32]):
            high = jnp.where(slot == j, roll(tile[:, Z - 128 :], 4 * j - 124, 1), high)
            low = jnp.where(slot == j, roll(tile[:, :128], 4 * j, 1), low)
        to_up(unit, high)
        to_down(unit, low)


def own_kernel(fields, z_up, z_down):
    tiles = [fields[f, x] for f in range(FIELDS) for x in range(X)]
    z_pack(tiles, z_up.__setitem__, z_down.__setitem__, iota((Y, 128), 1) // 4)


def rows_kernel(own_up, own_down, ym, yp, rows, z_up, z_down):
    _, _, in_ym, in_yp, _, _ = inside_flags()
    low_rows = iota((8, Z), 0) < 4
    for t in range(YPAIRS):
        minus, plus = ym[t], yp[t]
        plus, minus = plus * in_yp, minus * in_ym
        f, x = divmod(2 * t, X)
        rows[f, x] = jnp.where(low_rows, plus, roll(minus, 4, 0))
        rows[f, x + 1] = jnp.where(low_rows, roll(plus, 4, 0), minus)
    tiles = [rows[f, x] for f in range(FIELDS) for x in range(X)]
    ups, downs = {}, {}
    z_pack(tiles, ups.__setitem__, downs.__setitem__, iota((8, 128), 1) // 4)
    for unit in range(ZUNITS):
        z_up[unit, :Y], z_down[unit, :Y] = own_up[unit], own_down[unit]
        z_up[unit, Y:], z_down[unit, Y:] = ups[unit], downs[unit]


def third_kernel(rows, zm, zp, third, r_up, r_down):
    in_zm, in_zp = inside_flags()[4:]
    lane = iota((8, 128), 1)
    right = (lane < 4).astype(F32) * in_zp
    left = (lane >= 124).astype(F32) * in_zm
    slot = lane // 8
    row = iota((8, Z), 0)
    outer_rows = (row < 2) | (row >= 6)
    for f in range(FIELDS):
        for x in range(X):
            for h in range(3):
                unit, j = divmod(f * X + x, 32)
                cut = slice(8 * h, 8 * h + 8)
                plus, minus = roll(zp[unit, cut], -4 * j, 1), roll(zm[unit, cut], 124 - 4 * j, 1)
                third[f, x, cut] = plus * right + minus * left
    to_up, to_down = {}, {}
    for up, out in ((True, to_up), (False, to_down)):
        units = [jnp.zeros((8, 128), F32) for _ in range(4)]
        for i, (f, d) in enumerate(RELAYED):
            x = X - d if up else d - 1
            if (f, d) in SHARED:
                tile = rows[f, x]
                if d + 1 == CORNER[f]:
                    after = rows[f, x - 1 if up else x + 1]
                    tile = jnp.where(outer_rows, tile, roll(after, 4, 0))
                out[SHARED.index((f, d))] = tile
            for h in range(3):
                unit, j = divmod(3 * i + h, 16)
                tile = roll(third[f, x, 8 * h : 8 * h + 8], 8 * j + 4, 1)
                units[unit] = jnp.where(slot == j, tile, units[unit])
        for unit in range(0, 4, 2):
            out[len(SHARED) + unit // 2] = jnp.concatenate(units[unit : unit + 2], axis=1)
    for t in range(RTILES):
        r_up[t], r_down[t] = to_up[t], to_down[t]


def y_plus(a):
    return roll(a, -1, 0)


def y_minus(a):
    return roll(a, 1, 0)


def z_plus(a):
    return roll(a, -1, 1)


def z_minus(a):
    return roll(a, 1, 1)


def own(a):
    return a[:Y, :Z]


def cell_mask():
    _, _, in_ym, in_yp, in_zm, in_zp = inside_flags()
    row, col = iota((YE, ZE), 0), iota((YE, ZE), 1)
    in_y = jnp.where(row < Y, 1.0, jnp.where(row < Y + 4, in_yp, in_ym))
    in_z = jnp.where(
        col < Z, 1.0, jnp.where(col < Z + 4, in_zp, jnp.where(col >= ZE - 4, in_zm, 0.0))
    )
    return in_y * in_z


def beside(get, x):
    center = get(x)
    return [
        (get(x + 1), get(x - 1)),
        (y_plus(center), y_minus(center)),
        (z_plus(center), z_minus(center)),
    ]


def nearby(pairs):
    return sum(p + m for p, m in pairs)


def predicted(field, k, x):
    center = field(k, x)
    pairs = beside(lambda i: field(k, i), x)
    conv = 0.5 * sum(field(d, x) * (p - m) for d, (p, m) in enumerate(pairs))
    lap = nearby(pairs) - 6.0 * center
    return field(KEEP, x) * (center + DT * (field(VISC, x) * lap - conv))


def residual(field, pred, x, mask):
    div = 0.5 * (
        pred(0, x + 1)
        - pred(0, x - 1)
        + (y_plus(pred(1, x)) - y_minus(pred(1, x)))
        + (z_plus(pred(2, x)) - z_minus(pred(2, x)))
    )
    pairs = beside(lambda i: field(PRES, i), x)
    image = (6.0 + field(RELAX, x)) * field(PRES, x) - nearby(pairs)
    return (-div / DT - image) * mask, pairs


def image_of(field, get, x, mask):
    pairs = beside(get, x)
    return ((6.0 + field(RELAX, x)) * get(x) - nearby(pairs)) * mask, pairs


def first_part(field, pred, x, pairs, out, at):
    for d, (p, m) in enumerate(pairs):
        grad = own(p) - own(m)
        out[d, at] = own(field(KEEP, x)) * (own(pred(d, x)) - DT * 0.5 * grad)


def later_part(field, x, pairs, out, start, at):
    keep = own(field(KEEP, x)) * (-DT * 0.5)
    for d, (p, m) in enumerate(pairs):
        out[start + d, at] = keep * (own(p) - own(m))


def extended(fields, rows, third, f, x):
    return jnp.concatenate([jnp.concatenate([fields[f, x], rows[f, x]], axis=0), third[f, x]], axis=1)


def inner_kernel(fields, rows, third, pred_out, res_out, img_out, first_out, second_out):
    def field(f, x):
        return extended(fields, rows, third, f, x)

    def pred(k, x):
        return pred_out[k, x - 1]

    def res(x):
        return res_out[x - 2]

    mask = cell_mask()
    for x in range(1, 7):
        for k in range(3):
            pred_out[k, x - 1] = predicted(field, k, x)
    for x in range(2, 6):
        res_out[x - 2], pairs = residual(field, pred, x, mask)
        first_part(field, pred, x, pairs, first_out, x - 2)
    for x in range(3, 5):
        img_out[x - 3], pairs = image_of(field, res, x, mask)
        later_part(field, x, pairs, second_out, 0, x - 3)


def weight_kernel(host, off, z_high, z_low, xy):
    width = 256
    first = window_start()
    for c in range(host.shape[1] // width):
        cut = slice(c * width, c * width + width)
        place = iota((Z, width), 0) + lax.axis_index("prop") * Z
        weight = axis_weights(host, off, 2, cut, place)
        high = weight.astype(BF16)
        z_high[:, cut] = high
        z_low[:, cut] = (weight - high.astype(F32)).astype(BF16)
        place = iota((Y, width), 0) + position()[1] * Y
        weight = axis_weights(host, off, 1, cut, place)
        x_first = lax.axis_index("stream") * X + first
        for l in range(WINDOW):
            xy[l, :, cut] = weight * axis_weights(host, off, 0, cut, x_first + l)


def product(a, high, low, dims):
    a_high = a.astype(BF16)
    a_low = (a - a_high.astype(F32)).astype(BF16)

    def dot(p, q):
        return lax.dot_general(p, q, (dims, ((), ())), preferred_element_type=F32)

    return dot(a_low, high) + dot(a_high, low) + dot(a_high, high)


def main_kernel(
    fields,
    rows,
    third,
    xm,
    xp,
    rm,
    rp,
    pred_in,
    res_in,
    img_in,
    first_in,
    second_in,
    z_high,
    z_low,
    xy,
    keep_half,
    send_half,
    grads,
    r0_out,
    s_out,
    halo,
    pred_own,
    res_own,
    img_own,
    payload,
):
    in_xm, in_xp = inside_flags()[:2]

    lane = iota((8, 128), 1)
    ends = ((lane < 4) | (lane >= 124)).astype(F32)
    for side, (edge, relay, flag) in enumerate(((xm, rm, in_xm), (xp, rp, in_xp))):
        for i, layer in enumerate(XLAYERS):
            halo[side, i, :Y, :Z] = edge[i] * flag
            if layer not in RELAYED:
                halo[side, i, :Y, Z:] = jnp.zeros((Y, 128), F32)
                halo[side, i, Y:] = jnp.zeros((8, ZE), F32)
                continue
            n = RELAYED.index(layer)
            if layer in SHARED:
                tile = relay[SHARED.index(layer)]
            else:
                tile = roll(relay[SHARED.index((layer[0], layer[1] - 1))], 4, 0)
            halo[side, i, Y:, :Z] = tile * flag
            for h in range(3):
                unit, j = divmod(3 * n + h, 16)
                packed = relay[len(SHARED) + unit // 2, :, halves()[unit % 2]]
                halo[side, i, 8 * h : 8 * h + 8, Z:] = roll(packed, -8 * j - 4, 1) * (ends * flag)

    def field(f, x):
        if x < 0:
            return halo[0, XLAYERS.index((f, -x))]
        if x >= X:
            return halo[1, XLAYERS.index((f, x - X + 1))]
        return extended(fields, rows, third, f, x)

    def pred(k, x):
        return pred_in[k, x - 1] if 1 <= x < 7 else pred_own[k, x + 3]

    def res(x):
        return res_in[x - 2] if 2 <= x < 6 else res_own[x + 2]

    def img(x):
        return img_in[x - 3] if 3 <= x < 5 else img_own[x + 1]

    mask = cell_mask()
    masks = {x: mask * in_xm for x in (-2, -1)}
    masks.update({x: mask * in_xp for x in (X, X + 1)})
    for x in (-3, -2, -1, 0, 7, 8, 9, 10):
        for k in range(3 if -3 < x < X + 2 else 1):
            pred_own[k, x + 3] = predicted(field, k, x)
    for x in range(-2, X + 2):
        if not 2 <= x < 6:
            res_own[x + 2], pairs = residual(field, pred, x, masks.get(x, mask))
            if 0 <= x < X:
                first_part(field, pred, x, pairs, grads, x)
    grads[:3, 2:6] = first_in[...]
    for x in range(-1, X + 1):
        if not 3 <= x < 5:
            img_own[x + 1], pairs = image_of(field, res, x, masks.get(x, mask))
            if 0 <= x < X:
                later_part(field, x, pairs, grads, 3, x)
    grads[3:6, 3:5] = second_in[...]
    sums = [jnp.zeros((Y, Z), F32) for _ in range(4)]
    for x in range(X):
        image, pairs = image_of(field, img, x, 1.0)
        later_part(field, x, pairs, grads, 6, x)
        r, s = own(res(x)), own(img(x))
        r0_out[x], s_out[x] = r, s
        for i, (a, b) in enumerate(((r, r), (r, s), (s, s), (s, own(image)))):
            sums[i] = sums[i] + a * b
    payload[9] = jnp.zeros((8, 128), F32)
    for i, total in enumerate(sums):
        line = jnp.sum(total[:, :128] + total[:, 128:], axis=0, keepdims=True)
        payload[9, i : i + 1] = line

    samples = grads[:, pl.ds(window_start(), WINDOW)].reshape(9 * WINDOW * Y, Z)
    width = 256
    for c in range(z_high.shape[1] // width):
        cut = slice(c * width, c * width + width)
        parts = product(samples, z_high[:, cut], z_low[:, cut], ((1,), (0,)))
        parts = parts.reshape(9, WINDOW, Y, width)
        for k in range(9):
            total = sum(parts[k, l] * xy[l, :, cut] for l in range(WINDOW))
            line = jnp.sum(total, axis=0, keepdims=True)
            for half, piece in enumerate(halves(width)):
                at = c * (width // 128) + half
                payload[k, at : at + 1] = line[:, piece]
    second = lax.axis_index("core") == 1
    for k in range(5):
        keep_half[k] = jnp.where(second, payload[5 + k], payload[k])
        send_half[k] = jnp.where(second, payload[k], payload[5 + k])


def window_start():
    return jnp.where(lax.axis_index("stream") * X + X == 32, X - WINDOW, 0)


def axis_weights(host, off, d, cut, place):
    low = host[d : d + 1, cut]
    part = off[d : d + 1, cut]
    return jnp.where(place == low, 1.0 - part, 0.0) + jnp.where(place == low + 1, part, 0.0)


def final_kernel(
    mine,
    other,
    pres,
    grads,
    r0,
    s,
    z_high,
    z_low,
    xy,
    motion,
    coeff,
    velocity,
    pressure,
    points,
    force,
):
    second = lax.axis_index("core") == 1
    total = [jnp.where(second, other[k], mine[k]) for k in range(5)]
    total += [jnp.where(second, mine[k], other[k]) for k in range(5)]
    lines = total[9]
    rr, rs, ss, st = [jnp.sum(lines[i : i + 1], axis=1, keepdims=True) for i in range(4)]
    alpha = rr / rs
    new = rr - 2.0 * alpha * rs + alpha * alpha * ss
    beta = new / rr
    grow = 1.0 + beta
    curve = grow * grow * rs - 2.0 * grow * alpha * ss + alpha * alpha * st
    alpha2 = new / curve
    c0 = alpha + alpha2 * grow
    c1 = -alpha2 * alpha
    for k in range(3):
        value = total[k] + c0 * total[3 + k] + c1 * total[6 + k]
        for i in range(8):
            points[k : k + 1, i * 128 : i * 128 + 128] = value[i : i + 1]
    slip = points[...] - motion[...]
    speed = jnp.sqrt(jnp.sum(slip * slip, axis=0, keepdims=True) + 1.0)
    force[...] = (-DT * coeff[...] * speed) * slip
    for x in range(X):
        pressure[x] = pres[x] + c0 * r0[x] + c1 * s[x]
        for k in range(3):
            velocity[k, x] = grads[k, x] + c0 * grads[3 + k, x] + c1 * grads[6 + k, x]
    first = window_start()
    width = 256
    body = jnp.zeros((3 * WINDOW * Y, Z), F32)
    for c in range(z_high.shape[1] // width):
        cut = slice(c * width, c * width + width)
        scaled = jnp.concatenate(
            [xy[l, :, cut] * force[k : k + 1, cut] for k in range(3) for l in range(WINDOW)],
            axis=0,
        )
        body = body + product(scaled, z_high[:, cut], z_low[:, cut], ((1,), (1,)))
    body = body.reshape(3, WINDOW, Y, Z)
    for k in range(3):
        for l in range(WINDOW):
            velocity[k, first + l] = velocity[k, first + l] + body[k, l]


def exchange(up, down, axis, n):
    before = lax.ppermute(up, axis, [(i, (i + 1) % n) for i in range(n)])
    after = lax.ppermute(down, axis, [(i, (i - 1) % n) for i in range(n)])
    return before, after


def pairs_sum(value, axis, pairs):
    moves = [(a, b) for a, b in pairs] + [(b, a) for a, b in pairs]
    return value + lax.ppermute(value, axis, moves)


def swap_cores(value):
    return lax.ppermute(value, "core", [(0, 1), (1, 0)])


def total_over(value, axis, n):
    copies = jnp.broadcast_to(value[None], (n,) + value.shape)
    return jnp.sum(lax.all_to_all(copies, axis, 0, 0), axis=0)


def sds(*shape, dtype=F32):
    return jax.ShapeDtypeStruct(shape, dtype)


def call(kernel, outs, inputs, scratch=(), name=None, space=None, limit=16, us=1.0):
    return pl.pallas_call(
        kernel,
        out_shape=outs,
        in_specs=[pl.BlockSpec(memory_space=space or pltpu.VMEM)] * len(inputs),
        out_specs=[VMEM] * len(outs),
        scratch_shapes=scratch,
        compiler_params=pltpu.CompilerParams(vmem_limit_bytes=limit * MIB),
        cost_estimate=pl.CostEstimate(
            flops=0, bytes_accessed=int(us * 3.0e6), transcendentals=0
        ),
        name=name,
    )(*inputs)


def shards(
    velocity, eddy_visc, solid, pressure_old, relaxation, host_cell, offsets, blade_motion, force_coeff
):
    points = host_cell.shape[1]
    girth = ("gx", "core")
    block, side, edge = sds(X, Y, Z), sds(len(XLAYERS), Y, Z), sds(YPAIRS, 8, Z)
    fields, y_up, y_down, x_up, x_down = call(
        pack_kernel,
        (sds(FIELDS, X, Y, Z), edge, edge, side, side),
        [
            pltpu.with_memory_space_constraint(a, pltpu.HBM)
            for a in (velocity, eddy_visc, solid, pressure_old, relaxation)
        ],
        [pltpu.VMEM((X, Y, Z), jnp.int32), pltpu.SemaphoreType.DMA((5,))],
        name="pack",
        space=pltpu.HBM,
        limit=24,
    )
    from_y = exchange(y_up, y_down, girth, 8)
    from_x = exchange(x_up, x_down, "stream", 8)
    unit, own_unit = sds(ZUNITS, YE, 128), sds(ZUNITS, Y, 128)
    own_up, own_down = call(own_kernel, (own_unit, own_unit), (fields,), name="ownz", us=0.5)
    rows, z_up, z_down = call(
        rows_kernel, (sds(FIELDS, X, 8, Z), unit, unit), (own_up, own_down, *from_y), name="rows", us=0.1
    )
    from_z = exchange(z_up, z_down, "prop", 4)
    relay = sds(RTILES, 8, Z)
    third, r_up, r_down = call(
        third_kernel,
        (sds(FIELDS, X, YE, 128), relay, relay),
        (rows, *from_z),
        name="third",
        us=0.1,
    )
    wide = sds(Z, points, dtype=BF16)
    weights = call(
        weight_kernel, (wide, wide, sds(WINDOW, Y, points)), (host_cell, offsets), name="weights", us=0.5
    )
    inner = call(
        inner_kernel,
        (
            sds(3, 6, YE, ZE),
            sds(4, YE, ZE),
            sds(2, YE, ZE),
            sds(3, 4, Y, Z),
            sds(3, 2, Y, Z),
        ),
        (fields, rows, third),
        name="inner",
        us=1.5,
    )
    from_r = exchange(r_up, r_down, "stream", 8)
    half = sds(5, 8, 128)
    kept, sent, grads, r0, s = call(
        main_kernel,
        (half, half, sds(9, X, Y, Z), block, block),
        (fields, rows, third, *from_x, *from_r, *inner, *weights),
        [
            pltpu.VMEM((2, len(XLAYERS), YE, ZE), F32),
            pltpu.VMEM((3, X + 6, YE, ZE), F32),
            pltpu.VMEM((X + 4, YE, ZE), F32),
            pltpu.VMEM((X + 2, YE, ZE), F32),
            pltpu.VMEM((10, 8, 128), F32),
        ],
        name="main",
    )
    mine = kept + swap_cores(sent)
    mine = total_over(mine, ("gx", "prop"), 16)
    mine = pairs_sum(mine, "stream", [(0, 1), (2, 3), (4, 5), (6, 7)])
    mine = pairs_sum(mine, "stream", [(1, 2), (3, 4), (5, 6), (7, 0)])
    across = (3, 6, 5, 0, 7, 2, 1, 4)
    both = [(2 * i + c, 2 * across[i] + 1 - c) for i in range(8) for c in range(2)]
    other = swap_cores(mine) + lax.ppermute(mine, ("stream", "core"), both)
    mine = mine + lax.ppermute(mine, "stream", list(enumerate(across)))
    return call(
        final_kernel,
        (sds(3, X, Y, Z), block, sds(3, points)),
        (
            mine,
            other,
            pressure_old,
            grads,
            r0,
            s,
            *weights,
            blade_motion,
            force_coeff.reshape(1, points),
        ),
        [pltpu.VMEM((3, points), F32)],
        name="final",
    )


def solution(mesh):
    cut = Mesh(mesh.devices.reshape(8, 4, 2, 4), ("stream", "gx", "core", "prop"))
    cells = ("stream", ("gx", "core"), "prop")
    placed = (P(None, *cells),) + (P(*cells),) * 4 + (P(),) * 4
    return jax.shard_map(
        shards,
        mesh=cut,
        in_specs=placed,
        out_specs=(P(None, *cells), P(*cells), P()),
        check_vma=False,
    )
```

```python
import jax
import jax.numpy as jnp
from jax import lax
from jax.experimental import pallas as pl
from jax.experimental.pallas import tpu as pltpu
from jax.sharding import Mesh, PartitionSpec as P

DT = 0.1
F32 = jnp.float32
BF16 = jnp.bfloat16

X, Y, Z = 8, 16, 256
YE, ZE = 24, 384
VISC, KEEP, PRES, RELAX = 3, 4, 5, 6
FIELDS = 7
RADIUS = (4, 3, 3, 3, 3, 3, 2)
XLAYERS = [(f, d) for f in range(FIELDS) for d in range(1, RADIUS[f] + 1)]
CORNER = (3, 3, 3, 2, 2, 2, 1)
RELAYED = [(f, d) for f in range(FIELDS) for d in range(1, CORNER[f] + 1)]
SHARED = [(f, d) for f, d in RELAYED if d < CORNER[f]]
GIVEN = {(f, x) for f, d in RELAYED for x in (d - 1, X - d)}
YPAIRS = FIELDS * X // 2
ZUNITS = -(-FIELDS * X // 32)
SHARED += [(f, d) for f, d in RELAYED if CORNER[f] == 1]
RTILES = len(SHARED) + 2
WINDOW = 3
VMEM = pl.BlockSpec(memory_space=pltpu.VMEM)
MIB = 1024 * 1024


def iota(shape, dim):
    return lax.broadcasted_iota(jnp.int32, shape, dim)


def roll(a, shift, axis):
    shift = shift % a.shape[axis]
    return a if shift == 0 else pltpu.roll(a, shift, axis)


def halves(width=Z):
    return [slice(i, i + 128) for i in range(0, width, 128)]


def load(refs, own_out, stage, sems):
    velocity, visc, solid, pres, relax = refs
    copies = [
        pltpu.make_async_copy(velocity, own_out.at[:3], sems.at[0]),
        pltpu.make_async_copy(visc, own_out.at[VISC], sems.at[1]),
        pltpu.make_async_copy(solid, stage, sems.at[2]),
        pltpu.make_async_copy(pres, own_out.at[PRES], sems.at[3]),
        pltpu.make_async_copy(relax, own_out.at[RELAX], sems.at[4]),
    ]
    for copy in copies:
        copy.start()
    return {f: [copy] for f, copy in zip((0, VISC, KEEP, PRES, RELAX), copies)}


def pack_kernel(*args):
    refs, (fields, y_up, y_down, up, down, stage, sems) = args[:5], args[5:]
    copies = load(refs, fields, stage, sems)
    low_rows = iota((8, Z), 0) < 4
    for f in (VISC, PRES, RELAX, KEEP, 0, 1, 2):
        for copy in copies.get(f, ()):
            copy.wait()
        if f == KEEP:
            fields[KEEP] = 1.0 - stage[...].astype(F32)
        for x in range(0, X, 2):
            t = (f * X + x) // 2
            a, b = fields[f, x], fields[f, x + 1]
            y_up[t] = jnp.where(low_rows, roll(a[8:], 4, 0), b[8:])
            y_down[t] = jnp.where(low_rows, a[:8], roll(b[:8], 4, 0))
        for d in range(1, RADIUS[f] + 1):
            i = XLAYERS.index((f, d))
            up[i], down[i] = fields[f, X - d], fields[f, d - 1]


def position():
    return (
        lax.axis_index("stream"),
        lax.axis_index("gx") * 2 + lax.axis_index("core"),
        lax.axis_index("prop"),
    )


def inside_flags():
    out = []
    for i, n in zip(position(), (8, 8, 4)):
        out.append((i > 0).astype(F32))
        out.append((i < n - 1).astype(F32))
    return out


def z_pack(tiles, to_up, to_down, slot):
    for unit in range(ZUNITS):
        high = jnp.zeros(slot.shape, F32)
        low = jnp.zeros(slot.shape, F32)
        for j, tile in enumerate(tiles[32 * unit : 32 * unit + 32]):
            high = jnp.where(slot == j, roll(tile[:, Z - 128 :], 4 * j - 124, 1), high)
            low = jnp.where(slot == j, roll(tile[:, :128], 4 * j, 1), low)
        to_up(unit, high)
        to_down(unit, low)


def own_kernel(fields, z_up, z_down):
    tiles = [fields[f, x] for f in range(FIELDS) for x in range(X)]
    z_pack(tiles, z_up.__setitem__, z_down.__setitem__, iota((Y, 128), 1) // 4)


def rows_kernel(own_up, own_down, ym, yp, rows, z_up, z_down):
    _, _, in_ym, in_yp, _, _ = inside_flags()
    low_rows = iota((8, Z), 0) < 4
    for t in range(YPAIRS):
        minus, plus = ym[t], yp[t]
        plus, minus = plus * in_yp, minus * in_ym
        f, x = divmod(2 * t, X)
        rows[f, x] = jnp.where(low_rows, plus, roll(minus, 4, 0))
        rows[f, x + 1] = jnp.where(low_rows, roll(plus, 4, 0), minus)
    tiles = [rows[f, x] for f in range(FIELDS) for x in range(X)]
    ups, downs = {}, {}
    z_pack(tiles, ups.__setitem__, downs.__setitem__, iota((8, 128), 1) // 4)
    for unit in range(ZUNITS):
        z_up[unit, :Y], z_down[unit, :Y] = own_up[unit], own_down[unit]
        z_up[unit, Y:], z_down[unit, Y:] = ups[unit], downs[unit]


def z_halos(zm, zp, third, given):
    in_zm, in_zp = inside_flags()[4:]
    lane = iota((8, 128), 1)
    right = (lane < 4).astype(F32) * in_zp
    left = (lane >= 124).astype(F32) * in_zm
    for f in range(FIELDS):
        for x in range(X):
            if ((f, x) in GIVEN) != given:
                continue
            unit, j = divmod(f * X + x, 32)
            for h in range(3):
                cut = slice(8 * h, 8 * h + 8)
                plus, minus = roll(zp[unit, cut], -4 * j, 1), roll(zm[unit, cut], 124 - 4 * j, 1)
                third[f, x, cut] = plus * right + minus * left


def rest_kernel(zm, zp, third):
    z_halos(zm, zp, third, False)


def third_kernel(rows, zm, zp, third, r_up, r_down):
    z_halos(zm, zp, third, True)
    slot = iota((8, 128), 1) // 8
    row = iota((8, Z), 0)
    outer_rows = (row < 2) | (row >= 6)
    to_up, to_down = {}, {}
    for up, out in ((True, to_up), (False, to_down)):
        units = [jnp.zeros((8, 128), F32) for _ in range(4)]
        for i, (f, d) in enumerate(RELAYED):
            x = X - d if up else d - 1
            if (f, d) in SHARED:
                tile = rows[f, x]
                if d + 1 == CORNER[f]:
                    after = rows[f, x - 1 if up else x + 1]
                    tile = jnp.where(outer_rows, tile, roll(after, 4, 0))
                out[SHARED.index((f, d))] = tile
            for h in range(3):
                unit, j = divmod(3 * i + h, 16)
                tile = roll(third[f, x, 8 * h : 8 * h + 8], 8 * j + 4, 1)
                units[unit] = jnp.where(slot == j, tile, units[unit])
        for unit in range(0, 4, 2):
            out[len(SHARED) + unit // 2] = jnp.concatenate(units[unit : unit + 2], axis=1)
    for t in range(RTILES):
        r_up[t], r_down[t] = to_up[t], to_down[t]


def y_plus(a):
    return roll(a, -1, 0)


def y_minus(a):
    return roll(a, 1, 0)


def z_plus(a):
    return roll(a, -1, 1)


def z_minus(a):
    return roll(a, 1, 1)


def own(a):
    return a[:Y, :Z]


def cell_mask():
    _, _, in_ym, in_yp, in_zm, in_zp = inside_flags()
    row, col = iota((YE, ZE), 0), iota((YE, ZE), 1)
    in_y = jnp.where(row < Y, 1.0, jnp.where(row < Y + 4, in_yp, in_ym))
    in_z = jnp.where(
        col < Z, 1.0, jnp.where(col < Z + 4, in_zp, jnp.where(col >= ZE - 4, in_zm, 0.0))
    )
    return in_y * in_z


def beside(get, x):
    center = get(x)
    return [
        (get(x + 1), get(x - 1)),
        (y_plus(center), y_minus(center)),
        (z_plus(center), z_minus(center)),
    ]


def nearby(pairs):
    return sum(p + m for p, m in pairs)


def predicted(field, k, x):
    center = field(k, x)
    pairs = beside(lambda i: field(k, i), x)
    conv = 0.5 * sum(field(d, x) * (p - m) for d, (p, m) in enumerate(pairs))
    lap = nearby(pairs) - 6.0 * center
    return field(KEEP, x) * (center + DT * (field(VISC, x) * lap - conv))


def residual(field, pred, x, mask):
    div = 0.5 * (
        pred(0, x + 1)
        - pred(0, x - 1)
        + (y_plus(pred(1, x)) - y_minus(pred(1, x)))
        + (z_plus(pred(2, x)) - z_minus(pred(2, x)))
    )
    pairs = beside(lambda i: field(PRES, i), x)
    image = (6.0 + field(RELAX, x)) * field(PRES, x) - nearby(pairs)
    return (-div / DT - image) * mask, pairs


def image_of(field, get, x, mask):
    pairs = beside(get, x)
    return ((6.0 + field(RELAX, x)) * get(x) - nearby(pairs)) * mask, pairs


def first_part(field, pred, x, pairs, out, at):
    for d, (p, m) in enumerate(pairs):
        grad = own(p) - own(m)
        out[d, at] = own(field(KEEP, x)) * (own(pred(d, x)) - DT * 0.5 * grad)


def later_part(field, x, pairs, out, start, at):
    keep = own(field(KEEP, x)) * (-DT * 0.5)
    for d, (p, m) in enumerate(pairs):
        out[start + d, at] = keep * (own(p) - own(m))


def extended(fields, rows, third, rest, f, x):
    z_tile = third[f, x] if (f, x) in GIVEN else rest[f, x]
    return jnp.concatenate([jnp.concatenate([fields[f, x], rows[f, x]], axis=0), z_tile], axis=1)


def inner_kernel(fields, rows, third, rest, pred_out, res_out, img_out, first_out, second_out):
    def field(f, x):
        return extended(fields, rows, third, rest, f, x)

    def pred(k, x):
        return pred_out[k, x - 1]

    def res(x):
        return res_out[x - 2]

    mask = cell_mask()
    for x in range(1, 7):
        for k in range(3):
            pred_out[k, x - 1] = predicted(field, k, x)
    for x in range(2, 6):
        res_out[x - 2], pairs = residual(field, pred, x, mask)
        first_part(field, pred, x, pairs, first_out, x - 2)
    for x in range(3, 5):
        img_out[x - 3], pairs = image_of(field, res, x, mask)
        later_part(field, x, pairs, second_out, 0, x - 3)


def weight_kernel(host, off, z_high, z_low, xy):
    width = 256
    first = window_start()
    for c in range(host.shape[1] // width):
        cut = slice(c * width, c * width + width)
        place = iota((Z, width), 0) + lax.axis_index("prop") * Z
        weight = axis_weights(host, off, 2, cut, place)
        high = weight.astype(BF16)
        z_high[:, cut] = high
        z_low[:, cut] = (weight - high.astype(F32)).astype(BF16)
        place = iota((Y, width), 0) + position()[1] * Y
        weight = axis_weights(host, off, 1, cut, place)
        x_first = lax.axis_index("stream") * X + first
        for l in range(WINDOW):
            xy[l, :, cut] = weight * axis_weights(host, off, 0, cut, x_first + l)


def product(a, high, low, dims):
    a_high = a.astype(BF16)
    a_low = (a - a_high.astype(F32)).astype(BF16)

    def dot(p, q):
        return lax.dot_general(p, q, (dims, ((), ())), preferred_element_type=F32)

    return dot(a_low, high) + dot(a_high, low) + dot(a_high, high)


def main_kernel(
    fields,
    rows,
    third,
    rest,
    xm,
    xp,
    rm,
    rp,
    pred_in,
    res_in,
    img_in,
    first_in,
    second_in,
    z_high,
    z_low,
    xy,
    keep_half,
    send_half,
    grads,
    r0_out,
    s_out,
    halo,
    pred_own,
    res_own,
    img_own,
    payload,
):
    in_xm, in_xp = inside_flags()[:2]

    lane = iota((8, 128), 1)
    ends = ((lane < 4) | (lane >= 124)).astype(F32)
    for side, (edge, relay, flag) in enumerate(((xm, rm, in_xm), (xp, rp, in_xp))):
        for i, layer in enumerate(XLAYERS):
            halo[side, i, :Y, :Z] = edge[i] * flag
            if layer not in RELAYED:
                halo[side, i, :Y, Z:] = jnp.zeros((Y, 128), F32)
                halo[side, i, Y:] = jnp.zeros((8, ZE), F32)
                continue
            n = RELAYED.index(layer)
            if layer in SHARED:
                tile = relay[SHARED.index(layer)]
            else:
                tile = roll(relay[SHARED.index((layer[0], layer[1] - 1))], 4, 0)
            halo[side, i, Y:, :Z] = tile * flag
            for h in range(3):
                unit, j = divmod(3 * n + h, 16)
                packed = relay[len(SHARED) + unit // 2, :, halves()[unit % 2]]
                halo[side, i, 8 * h : 8 * h + 8, Z:] = roll(packed, -8 * j - 4, 1) * (ends * flag)

    def field(f, x):
        if x < 0:
            return halo[0, XLAYERS.index((f, -x))]
        if x >= X:
            return halo[1, XLAYERS.index((f, x - X + 1))]
        return extended(fields, rows, third, rest, f, x)

    def pred(k, x):
        return pred_in[k, x - 1] if 1 <= x < 7 else pred_own[k, x + 3]

    def res(x):
        return res_in[x - 2] if 2 <= x < 6 else res_own[x + 2]

    def img(x):
        return img_in[x - 3] if 3 <= x < 5 else img_own[x + 1]

    mask = cell_mask()
    masks = {x: mask * in_xm for x in (-2, -1)}
    masks.update({x: mask * in_xp for x in (X, X + 1)})
    for x in (-3, -2, -1, 0, 7, 8, 9, 10):
        for k in range(3 if -3 < x < X + 2 else 1):
            pred_own[k, x + 3] = predicted(field, k, x)
    for x in range(-2, X + 2):
        if not 2 <= x < 6:
            res_own[x + 2], pairs = residual(field, pred, x, masks.get(x, mask))
            if 0 <= x < X:
                first_part(field, pred, x, pairs, grads, x)
    grads[:3, 2:6] = first_in[...]
    for x in range(-1, X + 1):
        if not 3 <= x < 5:
            img_own[x + 1], pairs = image_of(field, res, x, masks.get(x, mask))
            if 0 <= x < X:
                later_part(field, x, pairs, grads, 3, x)
    grads[3:6, 3:5] = second_in[...]
    sums = [jnp.zeros((Y, Z), F32) for _ in range(4)]
    for x in range(X):
        image, pairs = image_of(field, img, x, 1.0)
        later_part(field, x, pairs, grads, 6, x)
        r, s = own(res(x)), own(img(x))
        r0_out[x], s_out[x] = r, s
        for i, (a, b) in enumerate(((r, r), (r, s), (s, s), (s, own(image)))):
            sums[i] = sums[i] + a * b
    payload[9] = jnp.zeros((8, 128), F32)
    for i, total in enumerate(sums):
        line = jnp.sum(total[:, :128] + total[:, 128:], axis=0, keepdims=True)
        payload[9, i : i + 1] = line

    samples = grads[:, pl.ds(window_start(), WINDOW)].reshape(9 * WINDOW * Y, Z)
    width = 256
    for c in range(z_high.shape[1] // width):
        cut = slice(c * width, c * width + width)
        parts = product(samples, z_high[:, cut], z_low[:, cut], ((1,), (0,)))
        parts = parts.reshape(9, WINDOW, Y, width)
        for k in range(9):
            total = sum(parts[k, l] * xy[l, :, cut] for l in range(WINDOW))
            line = jnp.sum(total, axis=0, keepdims=True)
            for half, piece in enumerate(halves(width)):
                at = c * (width // 128) + half
                payload[k, at : at + 1] = line[:, piece]
    second = lax.axis_index("core") == 1
    for k in range(5):
        keep_half[k] = jnp.where(second, payload[5 + k], payload[k])
        send_half[k] = jnp.where(second, payload[k], payload[5 + k])


def window_start():
    return jnp.where(lax.axis_index("stream") * X + X == 32, X - WINDOW, 0)


def axis_weights(host, off, d, cut, place):
    low = host[d : d + 1, cut]
    part = off[d : d + 1, cut]
    return jnp.where(place == low, 1.0 - part, 0.0) + jnp.where(place == low + 1, part, 0.0)


def final_kernel(
    mine,
    other,
    pres,
    grads,
    r0,
    s,
    z_high,
    z_low,
    xy,
    motion,
    coeff,
    velocity,
    pressure,
    points,
    force,
):
    second = lax.axis_index("core") == 1
    total = [jnp.where(second, other[k], mine[k]) for k in range(5)]
    total += [jnp.where(second, mine[k], other[k]) for k in range(5)]
    lines = total[9]
    rr, rs, ss, st = [jnp.sum(lines[i : i + 1], axis=1, keepdims=True) for i in range(4)]
    alpha = rr / rs
    new = rr - 2.0 * alpha * rs + alpha * alpha * ss
    beta = new / rr
    grow = 1.0 + beta
    curve = grow * grow * rs - 2.0 * grow * alpha * ss + alpha * alpha * st
    alpha2 = new / curve
    c0 = alpha + alpha2 * grow
    c1 = -alpha2 * alpha
    for k in range(3):
        value = total[k] + c0 * total[3 + k] + c1 * total[6 + k]
        for i in range(8):
            points[k : k + 1, i * 128 : i * 128 + 128] = value[i : i + 1]
    slip = points[...] - motion[...]
    speed = jnp.sqrt(jnp.sum(slip * slip, axis=0, keepdims=True) + 1.0)
    force[...] = (-DT * coeff[...] * speed) * slip
    for x in range(X):
        pressure[x] = pres[x] + c0 * r0[x] + c1 * s[x]
        for k in range(3):
            velocity[k, x] = grads[k, x] + c0 * grads[3 + k, x] + c1 * grads[6 + k, x]
    first = window_start()
    width = 256
    body = jnp.zeros((3 * WINDOW * Y, Z), F32)
    for c in range(z_high.shape[1] // width):
        cut = slice(c * width, c * width + width)
        scaled = jnp.concatenate(
            [xy[l, :, cut] * force[k : k + 1, cut] for k in range(3) for l in range(WINDOW)],
            axis=0,
        )
        body = body + product(scaled, z_high[:, cut], z_low[:, cut], ((1,), (1,)))
    body = body.reshape(3, WINDOW, Y, Z)
    for k in range(3):
        for l in range(WINDOW):
            velocity[k, first + l] = velocity[k, first + l] + body[k, l]


def exchange(up, down, axis, n):
    before = lax.ppermute(up, axis, [(i, (i + 1) % n) for i in range(n)])
    after = lax.ppermute(down, axis, [(i, (i - 1) % n) for i in range(n)])
    return before, after


def pairs_sum(value, axis, pairs):
    moves = [(a, b) for a, b in pairs] + [(b, a) for a, b in pairs]
    return value + lax.ppermute(value, axis, moves)


def swap_cores(value):
    return lax.ppermute(value, "core", [(0, 1), (1, 0)])


def total_over(value, axis, n):
    copies = jnp.broadcast_to(value[None], (n,) + value.shape)
    return jnp.sum(lax.all_to_all(copies, axis, 0, 0), axis=0)


def sds(*shape, dtype=F32):
    return jax.ShapeDtypeStruct(shape, dtype)


def call(kernel, outs, inputs, scratch=(), name=None, space=None, limit=16, us=1.0):
    return pl.pallas_call(
        kernel,
        out_shape=outs,
        in_specs=[pl.BlockSpec(memory_space=space or pltpu.VMEM)] * len(inputs),
        out_specs=[VMEM] * len(outs),
        scratch_shapes=scratch,
        compiler_params=pltpu.CompilerParams(vmem_limit_bytes=limit * MIB),
        cost_estimate=pl.CostEstimate(
            flops=0, bytes_accessed=int(us * 3.0e6), transcendentals=0
        ),
        name=name,
    )(*inputs)


def shards(
    velocity, eddy_visc, solid, pressure_old, relaxation, host_cell, offsets, blade_motion, force_coeff
):
    points = host_cell.shape[1]
    girth = ("gx", "core")
    block, side, edge = sds(X, Y, Z), sds(len(XLAYERS), Y, Z), sds(YPAIRS, 8, Z)
    fields, y_up, y_down, x_up, x_down = call(
        pack_kernel,
        (sds(FIELDS, X, Y, Z), edge, edge, side, side),
        [
            pltpu.with_memory_space_constraint(a, pltpu.HBM)
            for a in (velocity, eddy_visc, solid, pressure_old, relaxation)
        ],
        [pltpu.VMEM((X, Y, Z), jnp.int32), pltpu.SemaphoreType.DMA((5,))],
        name="pack",
        space=pltpu.HBM,
        limit=24,
    )
    from_y = exchange(y_up, y_down, girth, 8)
    from_x = exchange(x_up, x_down, "stream", 8)
    unit, own_unit = sds(ZUNITS, YE, 128), sds(ZUNITS, Y, 128)
    own_up, own_down = call(own_kernel, (own_unit, own_unit), (fields,), name="ownz", us=0.5)
    rows, z_up, z_down = call(
        rows_kernel, (sds(FIELDS, X, 8, Z), unit, unit), (own_up, own_down, *from_y), name="rows", us=0.1
    )
    from_z = exchange(z_up, z_down, "prop", 4)
    relay = sds(RTILES, 8, Z)
    third, r_up, r_down = call(
        third_kernel,
        (sds(FIELDS, X, YE, 128), relay, relay),
        (rows, *from_z),
        name="third",
        us=0.1,
    )
    wide = sds(Z, points, dtype=BF16)
    weights = call(
        weight_kernel, (wide, wide, sds(WINDOW, Y, points)), (host_cell, offsets), name="weights", us=0.5
    )
    rest = call(rest_kernel, (sds(FIELDS, X, YE, 128),), from_z, name="rest", us=0.3)[0]
    inner = call(
        inner_kernel,
        (
            sds(3, 6, YE, ZE),
            sds(4, YE, ZE),
            sds(2, YE, ZE),
            sds(3, 4, Y, Z),
            sds(3, 2, Y, Z),
        ),
        (fields, rows, third, rest),
        name="inner",
        us=1.5,
    )
    from_r = exchange(r_up, r_down, "stream", 8)
    half = sds(5, 8, 128)
    kept, sent, grads, r0, s = call(
        main_kernel,
        (half, half, sds(9, X, Y, Z), block, block),
        (fields, rows, third, rest, *from_x, *from_r, *inner, *weights),
        [
            pltpu.VMEM((2, len(XLAYERS), YE, ZE), F32),
            pltpu.VMEM((3, X + 6, YE, ZE), F32),
            pltpu.VMEM((X + 4, YE, ZE), F32),
            pltpu.VMEM((X + 2, YE, ZE), F32),
            pltpu.VMEM((10, 8, 128), F32),
        ],
        name="main",
    )
    mine = kept + swap_cores(sent)
    mine = total_over(mine, ("gx", "prop"), 16)
    mine = pairs_sum(mine, "stream", [(0, 1), (2, 3), (4, 5), (6, 7)])
    mine = pairs_sum(mine, "stream", [(1, 2), (3, 4), (5, 6), (7, 0)])
    across = (3, 6, 5, 0, 7, 2, 1, 4)
    both = [(2 * i + c, 2 * across[i] + 1 - c) for i in range(8) for c in range(2)]
    other = swap_cores(mine) + lax.ppermute(mine, ("stream", "core"), both)
    mine = mine + lax.ppermute(mine, "stream", list(enumerate(across)))
    return call(
        final_kernel,
        (sds(3, X, Y, Z), block, sds(3, points)),
        (
            mine,
            other,
            pressure_old,
            grads,
            r0,
            s,
            *weights,
            blade_motion,
            force_coeff.reshape(1, points),
        ),
        [pltpu.VMEM((3, points), F32)],
        name="final",
    )


def solution(mesh):
    cut = Mesh(mesh.devices.reshape(8, 4, 2, 4), ("stream", "gx", "core", "prop"))
    cells = ("stream", ("gx", "core"), "prop")
    placed = (P(None, *cells),) + (P(*cells),) * 4 + (P(),) * 4
    return jax.shard_map(
        shards,
        mesh=cut,
        in_specs=placed,
        out_specs=(P(None, *cells), P(*cells), P()),
        check_vma=False,
    )
```

```python
import jax
import jax.numpy as jnp
from jax import lax
from jax.experimental import pallas as pl
from jax.experimental.pallas import tpu as pltpu
from jax.sharding import Mesh, PartitionSpec as P

DT = 0.1
F32 = jnp.float32
BF16 = jnp.bfloat16

X, Y, Z = 8, 16, 256
YE, ZE = 24, 384
VISC, KEEP, PRES, RELAX = 3, 4, 5, 6
FIELDS = 7
RADIUS = (4, 3, 3, 3, 3, 3, 2)
XLAYERS = [(f, d) for f in range(FIELDS) for d in range(1, RADIUS[f] + 1)]
CORNER = (3, 3, 3, 2, 2, 2, 1)
RELAYED = [(f, d) for f in range(FIELDS) for d in range(1, CORNER[f] + 1)]
SHARED = [(f, d) for f, d in RELAYED if d < CORNER[f]]
GIVEN = {(f, x) for f, d in RELAYED for x in (d - 1, X - d)}
YPAIRS = FIELDS * X // 2
ZUNITS = -(-FIELDS * X // 32)
RTILES = len(SHARED) + 2
WINDOW = 3
VMEM = pl.BlockSpec(memory_space=pltpu.VMEM)
MIB = 1024 * 1024


def iota(shape, dim):
    return lax.broadcasted_iota(jnp.int32, shape, dim)


def roll(a, shift, axis):
    shift = shift % a.shape[axis]
    return a if shift == 0 else pltpu.roll(a, shift, axis)


def halves(width=Z):
    return [slice(i, i + 128) for i in range(0, width, 128)]


def load(refs, own_out, stage, sems):
    velocity, visc, solid, pres, relax = refs
    copies = [
        pltpu.make_async_copy(velocity, own_out.at[:3], sems.at[0]),
        pltpu.make_async_copy(visc, own_out.at[VISC], sems.at[1]),
        pltpu.make_async_copy(solid, stage, sems.at[2]),
        pltpu.make_async_copy(pres, own_out.at[PRES], sems.at[3]),
        pltpu.make_async_copy(relax, own_out.at[RELAX], sems.at[4]),
    ]
    for copy in copies:
        copy.start()
    return {f: [copy] for f, copy in zip((0, VISC, KEEP, PRES, RELAX), copies)}


def pack_kernel(*args):
    refs, (fields, y_up, y_down, up, down, stage, sems) = args[:5], args[5:]
    copies = load(refs, fields, stage, sems)
    low_rows = iota((8, Z), 0) < 4
    for f in (VISC, PRES, RELAX, KEEP, 0, 1, 2):
        for copy in copies.get(f, ()):
            copy.wait()
        if f == KEEP:
            fields[KEEP] = 1.0 - stage[...].astype(F32)
        for x in range(0, X, 2):
            t = (f * X + x) // 2
            a, b = fields[f, x], fields[f, x + 1]
            y_up[t] = jnp.where(low_rows, roll(a[8:], 4, 0), b[8:])
            y_down[t] = jnp.where(low_rows, a[:8], roll(b[:8], 4, 0))
        for d in range(1, RADIUS[f] + 1):
            i = XLAYERS.index((f, d))
            up[i], down[i] = fields[f, X - d], fields[f, d - 1]


def position():
    return (
        lax.axis_index("stream"),
        lax.axis_index("gx") * 2 + lax.axis_index("core"),
        lax.axis_index("prop"),
    )


def inside_flags():
    out = []
    for i, n in zip(position(), (8, 8, 4)):
        out.append((i > 0).astype(F32))
        out.append((i < n - 1).astype(F32))
    return out


def z_pack(tiles, to_up, to_down, slot):
    for unit in range(ZUNITS):
        high = jnp.zeros(slot.shape, F32)
        low = jnp.zeros(slot.shape, F32)
        for j, tile in enumerate(tiles[32 * unit : 32 * unit + 32]):
            high = jnp.where(slot == j, roll(tile[:, Z - 128 :], 4 * j - 124, 1), high)
            low = jnp.where(slot == j, roll(tile[:, :128], 4 * j, 1), low)
        to_up(unit, high)
        to_down(unit, low)


def own_kernel(fields, z_up, z_down):
    tiles = [fields[f, x] for f in range(FIELDS) for x in range(X)]
    z_pack(tiles, z_up.__setitem__, z_down.__setitem__, iota((Y, 128), 1) // 4)


def rows_kernel(own_up, own_down, ym, yp, rows, z_up, z_down):
    _, _, in_ym, in_yp, _, _ = inside_flags()
    low_rows = iota((8, Z), 0) < 4
    for t in range(YPAIRS):
        minus, plus = ym[t], yp[t]
        plus, minus = plus * in_yp, minus * in_ym
        f, x = divmod(2 * t, X)
        rows[f, x] = jnp.where(low_rows, plus, roll(minus, 4, 0))
        rows[f, x + 1] = jnp.where(low_rows, roll(plus, 4, 0), minus)
    tiles = [rows[f, x] for f in range(FIELDS) for x in range(X)]
    ups, downs = {}, {}
    z_pack(tiles, ups.__setitem__, downs.__setitem__, iota((8, 128), 1) // 4)
    for unit in range(ZUNITS):
        z_up[unit, :Y], z_down[unit, :Y] = own_up[unit], own_down[unit]
        z_up[unit, Y:], z_down[unit, Y:] = ups[unit], downs[unit]


def z_halos(zm, zp, third, given):
    in_zm, in_zp = inside_flags()[4:]
    lane = iota((8, 128), 1)
    right = (lane < 4).astype(F32) * in_zp
    left = (lane >= 124).astype(F32) * in_zm
    for f in range(FIELDS):
        for x in range(X):
            if ((f, x) in GIVEN) != given:
                continue
            unit, j = divmod(f * X + x, 32)
            for h in range(3):
                cut = slice(8 * h, 8 * h + 8)
                plus, minus = roll(zp[unit, cut], -4 * j, 1), roll(zm[unit, cut], 124 - 4 * j, 1)
                third[f, x, cut] = plus * right + minus * left


def rest_kernel(zm, zp, third):
    z_halos(zm, zp, third, False)


def third_kernel(rows, zm, zp, third, r_up, r_down):
    z_halos(zm, zp, third, True)
    slot = iota((8, 128), 1) // 8
    row = iota((8, Z), 0)
    outer_rows = (row < 2) | (row >= 6)
    to_up, to_down = {}, {}
    for up, out in ((True, to_up), (False, to_down)):
        units = [jnp.zeros((8, 128), F32) for _ in range(4)]
        for i, (f, d) in enumerate(RELAYED):
            x = X - d if up else d - 1
            if (f, d) in SHARED:
                tile = rows[f, x]
                if d + 1 == CORNER[f]:
                    after = rows[f, x - 1 if up else x + 1]
                    tile = jnp.where(outer_rows, tile, roll(after, 4, 0))
                if (f, d) == SHARED[0]:
                    tile = jnp.where((row == 3) | (row == 4), roll(rows[RELAX, x], 4, 0), tile)
                out[SHARED.index((f, d))] = tile
            for h in range(3):
                unit, j = divmod(3 * i + h, 16)
                tile = roll(third[f, x, 8 * h : 8 * h + 8], 8 * j + 4, 1)
                units[unit] = jnp.where(slot == j, tile, units[unit])
        for unit in range(0, 4, 2):
            out[len(SHARED) + unit // 2] = jnp.concatenate(units[unit : unit + 2], axis=1)
    for t in range(RTILES):
        r_up[t], r_down[t] = to_up[t], to_down[t]


def y_plus(a):
    return roll(a, -1, 0)


def y_minus(a):
    return roll(a, 1, 0)


def z_plus(a):
    return roll(a, -1, 1)


def z_minus(a):
    return roll(a, 1, 1)


def own(a):
    return a[:Y, :Z]


def cell_mask():
    _, _, in_ym, in_yp, in_zm, in_zp = inside_flags()
    row, col = iota((YE, ZE), 0), iota((YE, ZE), 1)
    in_y = jnp.where(row < Y, 1.0, jnp.where(row < Y + 4, in_yp, in_ym))
    in_z = jnp.where(
        col < Z, 1.0, jnp.where(col < Z + 4, in_zp, jnp.where(col >= ZE - 4, in_zm, 0.0))
    )
    return in_y * in_z


def beside(get, x):
    center = get(x)
    return [
        (get(x + 1), get(x - 1)),
        (y_plus(center), y_minus(center)),
        (z_plus(center), z_minus(center)),
    ]


def nearby(pairs):
    return sum(p + m for p, m in pairs)


def predicted(field, k, x):
    center = field(k, x)
    pairs = beside(lambda i: field(k, i), x)
    conv = 0.5 * sum(field(d, x) * (p - m) for d, (p, m) in enumerate(pairs))
    lap = nearby(pairs) - 6.0 * center
    return field(KEEP, x) * (center + DT * (field(VISC, x) * lap - conv))


def residual(field, pred, x, mask):
    div = 0.5 * (
        pred(0, x + 1)
        - pred(0, x - 1)
        + (y_plus(pred(1, x)) - y_minus(pred(1, x)))
        + (z_plus(pred(2, x)) - z_minus(pred(2, x)))
    )
    pairs = beside(lambda i: field(PRES, i), x)
    image = (6.0 + field(RELAX, x)) * field(PRES, x) - nearby(pairs)
    return (-div / DT - image) * mask, pairs


def image_of(field, get, x, mask):
    pairs = beside(get, x)
    return ((6.0 + field(RELAX, x)) * get(x) - nearby(pairs)) * mask, pairs


def first_part(field, pred, x, pairs, out, at):
    for d, (p, m) in enumerate(pairs):
        grad = own(p) - own(m)
        out[d, at] = own(field(KEEP, x)) * (own(pred(d, x)) - DT * 0.5 * grad)


def later_part(field, x, pairs, out, start, at):
    keep = own(field(KEEP, x)) * (-DT * 0.5)
    for d, (p, m) in enumerate(pairs):
        out[start + d, at] = keep * (own(p) - own(m))


def extended(fields, rows, third, rest, f, x):
    z_tile = third[f, x] if (f, x) in GIVEN else rest[f, x]
    return jnp.concatenate([jnp.concatenate([fields[f, x], rows[f, x]], axis=0), z_tile], axis=1)


def inner_kernel(fields, rows, third, rest, pred_out, res_out, img_out, first_out, second_out):
    def field(f, x):
        return extended(fields, rows, third, rest, f, x)

    def pred(k, x):
        return pred_out[k, x - 1]

    def res(x):
        return res_out[x - 2]

    mask = cell_mask()
    for x in range(1, 7):
        for k in range(3):
            pred_out[k, x - 1] = predicted(field, k, x)
    for x in range(2, 6):
        res_out[x - 2], pairs = residual(field, pred, x, mask)
        first_part(field, pred, x, pairs, first_out, x - 2)
    for x in range(3, 5):
        img_out[x - 3], pairs = image_of(field, res, x, mask)
        later_part(field, x, pairs, second_out, 0, x - 3)


def weight_kernel(host, off, z_high, z_low, xy):
    width = 256
    first = window_start()
    for c in range(host.shape[1] // width):
        cut = slice(c * width, c * width + width)
        place = iota((Z, width), 0) + lax.axis_index("prop") * Z
        weight = axis_weights(host, off, 2, cut, place)
        high = weight.astype(BF16)
        z_high[:, cut] = high
        z_low[:, cut] = (weight - high.astype(F32)).astype(BF16)
        place = iota((Y, width), 0) + position()[1] * Y
        weight = axis_weights(host, off, 1, cut, place)
        x_first = lax.axis_index("stream") * X + first
        for l in range(WINDOW):
            xy[l, :, cut] = weight * axis_weights(host, off, 0, cut, x_first + l)


def product(a, high, low, dims):
    a_high = a.astype(BF16)
    a_low = (a - a_high.astype(F32)).astype(BF16)

    def dot(p, q):
        return lax.dot_general(p, q, (dims, ((), ())), preferred_element_type=F32)

    return dot(a_low, high) + dot(a_high, low) + dot(a_high, high)


def main_kernel(
    fields,
    rows,
    third,
    rest,
    xm,
    xp,
    rm,
    rp,
    pred_in,
    res_in,
    img_in,
    first_in,
    second_in,
    z_high,
    z_low,
    xy,
    keep_half,
    send_half,
    grads,
    r0_out,
    s_out,
    halo,
    pred_own,
    res_own,
    img_own,
    payload,
):
    in_xm, in_xp = inside_flags()[:2]

    lane = iota((8, 128), 1)
    ends = ((lane < 4) | (lane >= 124)).astype(F32)
    for side, (edge, relay, flag) in enumerate(((xm, rm, in_xm), (xp, rp, in_xp))):
        for i, layer in enumerate(XLAYERS):
            halo[side, i, :Y, :Z] = edge[i] * flag
            if layer not in RELAYED:
                halo[side, i, :Y, Z:] = jnp.zeros((Y, 128), F32)
                halo[side, i, Y:] = jnp.zeros((8, ZE), F32)
                continue
            n = RELAYED.index(layer)
            if layer in SHARED:
                tile = relay[SHARED.index(layer)]
            else:
                host = SHARED[0] if layer[0] == RELAX else (layer[0], layer[1] - 1)
                tile = roll(relay[SHARED.index(host)], 4, 0)
            halo[side, i, Y:, :Z] = tile * flag
            for h in range(3):
                unit, j = divmod(3 * n + h, 16)
                packed = relay[len(SHARED) + unit // 2, :, halves()[unit % 2]]
                halo[side, i, 8 * h : 8 * h + 8, Z:] = roll(packed, -8 * j - 4, 1) * (ends * flag)

    def field(f, x):
        if x < 0:
            return halo[0, XLAYERS.index((f, -x))]
        if x >= X:
            return halo[1, XLAYERS.index((f, x - X + 1))]
        return extended(fields, rows, third, rest, f, x)

    def pred(k, x):
        return pred_in[k, x - 1] if 1 <= x < 7 else pred_own[k, x + 3]

    def res(x):
        return res_in[x - 2] if 2 <= x < 6 else res_own[x + 2]

    def img(x):
        return img_in[x - 3] if 3 <= x < 5 else img_own[x + 1]

    mask = cell_mask()
    masks = {x: mask * in_xm for x in (-2, -1)}
    masks.update({x: mask * in_xp for x in (X, X + 1)})
    for x in (-3, -2, -1, 0, 7, 8, 9, 10):
        for k in range(3 if -3 < x < X + 2 else 1):
            pred_own[k, x + 3] = predicted(field, k, x)
    for x in range(-2, X + 2):
        if not 2 <= x < 6:
            res_own[x + 2], pairs = residual(field, pred, x, masks.get(x, mask))
            if 0 <= x < X:
                first_part(field, pred, x, pairs, grads, x)
    grads[:3, 2:6] = first_in[...]
    for x in range(-1, X + 1):
        if not 3 <= x < 5:
            img_own[x + 1], pairs = image_of(field, res, x, masks.get(x, mask))
            if 0 <= x < X:
                later_part(field, x, pairs, grads, 3, x)
    grads[3:6, 3:5] = second_in[...]
    sums = [jnp.zeros((Y, Z), F32) for _ in range(4)]
    for x in range(X):
        image, pairs = image_of(field, img, x, 1.0)
        later_part(field, x, pairs, grads, 6, x)
        r, s = own(res(x)), own(img(x))
        r0_out[x], s_out[x] = r, s
        for i, (a, b) in enumerate(((r, r), (r, s), (s, s), (s, own(image)))):
            sums[i] = sums[i] + a * b
    payload[9] = jnp.zeros((8, 128), F32)
    for i, total in enumerate(sums):
        line = jnp.sum(total[:, :128] + total[:, 128:], axis=0, keepdims=True)
        payload[9, i : i + 1] = line

    samples = grads[:, pl.ds(window_start(), WINDOW)].reshape(9 * WINDOW * Y, Z)
    width = 256
    for c in range(z_high.shape[1] // width):
        cut = slice(c * width, c * width + width)
        parts = product(samples, z_high[:, cut], z_low[:, cut], ((1,), (0,)))
        parts = parts.reshape(9, WINDOW, Y, width)
        for k in range(9):
            total = sum(parts[k, l] * xy[l, :, cut] for l in range(WINDOW))
            line = jnp.sum(total, axis=0, keepdims=True)
            for half, piece in enumerate(halves(width)):
                at = c * (width // 128) + half
                payload[k, at : at + 1] = line[:, piece]
    second = lax.axis_index("core") == 1
    for k in range(5):
        keep_half[k] = jnp.where(second, payload[5 + k], payload[k])
        send_half[k] = jnp.where(second, payload[k], payload[5 + k])


def window_start():
    return jnp.where(lax.axis_index("stream") * X + X == 32, X - WINDOW, 0)


def axis_weights(host, off, d, cut, place):
    low = host[d : d + 1, cut]
    part = off[d : d + 1, cut]
    return jnp.where(place == low, 1.0 - part, 0.0) + jnp.where(place == low + 1, part, 0.0)


def final_kernel(
    mine,
    other,
    pres,
    grads,
    r0,
    s,
    z_high,
    z_low,
    xy,
    motion,
    coeff,
    velocity,
    pressure,
    points,
    force,
):
    second = lax.axis_index("core") == 1
    total = [jnp.where(second, other[k], mine[k]) for k in range(5)]
    total += [jnp.where(second, mine[k], other[k]) for k in range(5)]
    lines = total[9]
    rr, rs, ss, st = [jnp.sum(lines[i : i + 1], axis=1, keepdims=True) for i in range(4)]
    alpha = rr / rs
    new = rr - 2.0 * alpha * rs + alpha * alpha * ss
    beta = new / rr
    grow = 1.0 + beta
    curve = grow * grow * rs - 2.0 * grow * alpha * ss + alpha * alpha * st
    alpha2 = new / curve
    c0 = alpha + alpha2 * grow
    c1 = -alpha2 * alpha
    for k in range(3):
        value = total[k] + c0 * total[3 + k] + c1 * total[6 + k]
        for i in range(8):
            points[k : k + 1, i * 128 : i * 128 + 128] = value[i : i + 1]
    slip = points[...] - motion[...]
    speed = jnp.sqrt(jnp.sum(slip * slip, axis=0, keepdims=True) + 1.0)
    force[...] = (-DT * coeff[...] * speed) * slip
    for x in range(X):
        pressure[x] = pres[x] + c0 * r0[x] + c1 * s[x]
        for k in range(3):
            velocity[k, x] = grads[k, x] + c0 * grads[3 + k, x] + c1 * grads[6 + k, x]
    first = window_start()
    width = 256
    body = jnp.zeros((3 * WINDOW * Y, Z), F32)
    for c in range(z_high.shape[1] // width):
        cut = slice(c * width, c * width + width)
        scaled = jnp.concatenate(
            [xy[l, :, cut] * force[k : k + 1, cut] for k in range(3) for l in range(WINDOW)],
            axis=0,
        )
        body = body + product(scaled, z_high[:, cut], z_low[:, cut], ((1,), (1,)))
    body = body.reshape(3, WINDOW, Y, Z)
    for k in range(3):
        for l in range(WINDOW):
            velocity[k, first + l] = velocity[k, first + l] + body[k, l]


def exchange(up, down, axis, n):
    before = lax.ppermute(up, axis, [(i, (i + 1) % n) for i in range(n)])
    after = lax.ppermute(down, axis, [(i, (i - 1) % n) for i in range(n)])
    return before, after


def pairs_sum(value, axis, pairs):
    moves = [(a, b) for a, b in pairs] + [(b, a) for a, b in pairs]
    return value + lax.ppermute(value, axis, moves)


def swap_cores(value):
    return lax.ppermute(value, "core", [(0, 1), (1, 0)])


def total_over(value, axis, n):
    copies = jnp.broadcast_to(value[None], (n,) + value.shape)
    return jnp.sum(lax.all_to_all(copies, axis, 0, 0), axis=0)


def sds(*shape, dtype=F32):
    return jax.ShapeDtypeStruct(shape, dtype)


def call(kernel, outs, inputs, scratch=(), name=None, space=None, limit=16, us=1.0):
    return pl.pallas_call(
        kernel,
        out_shape=outs,
        in_specs=[pl.BlockSpec(memory_space=space or pltpu.VMEM)] * len(inputs),
        out_specs=[VMEM] * len(outs),
        scratch_shapes=scratch,
        compiler_params=pltpu.CompilerParams(vmem_limit_bytes=limit * MIB),
        cost_estimate=pl.CostEstimate(
            flops=0, bytes_accessed=int(us * 3.0e6), transcendentals=0
        ),
        name=name,
    )(*inputs)


def shards(
    velocity, eddy_visc, solid, pressure_old, relaxation, host_cell, offsets, blade_motion, force_coeff
):
    points = host_cell.shape[1]
    girth = ("gx", "core")
    block, side, edge = sds(X, Y, Z), sds(len(XLAYERS), Y, Z), sds(YPAIRS, 8, Z)
    fields, y_up, y_down, x_up, x_down = call(
        pack_kernel,
        (sds(FIELDS, X, Y, Z), edge, edge, side, side),
        [
            pltpu.with_memory_space_constraint(a, pltpu.HBM)
            for a in (velocity, eddy_visc, solid, pressure_old, relaxation)
        ],
        [pltpu.VMEM((X, Y, Z), jnp.int32), pltpu.SemaphoreType.DMA((5,))],
        name="pack",
        space=pltpu.HBM,
        limit=24,
    )
    from_y = exchange(y_up, y_down, girth, 8)
    from_x = exchange(x_up, x_down, "stream", 8)
    unit, own_unit = sds(ZUNITS, YE, 128), sds(ZUNITS, Y, 128)
    own_up, own_down = call(own_kernel, (own_unit, own_unit), (fields,), name="ownz", us=0.5)
    rows, z_up, z_down = call(
        rows_kernel, (sds(FIELDS, X, 8, Z), unit, unit), (own_up, own_down, *from_y), name="rows", us=0.1
    )
    from_z = exchange(z_up, z_down, "prop", 4)
    relay = sds(RTILES, 8, Z)
    third, r_up, r_down = call(
        third_kernel,
        (sds(FIELDS, X, YE, 128), relay, relay),
        (rows, *from_z),
        name="third",
        us=0.1,
    )
    wide = sds(Z, points, dtype=BF16)
    weights = call(
        weight_kernel, (wide, wide, sds(WINDOW, Y, points)), (host_cell, offsets), name="weights", us=0.5
    )
    rest = call(rest_kernel, (sds(FIELDS, X, YE, 128),), from_z, name="rest", us=0.3)[0]
    inner = call(
        inner_kernel,
        (
            sds(3, 6, YE, ZE),
            sds(4, YE, ZE),
            sds(2, YE, ZE),
            sds(3, 4, Y, Z),
            sds(3, 2, Y, Z),
        ),
        (fields, rows, third, rest),
        name="inner",
        us=1.5,
    )
    from_r = exchange(r_up, r_down, "stream", 8)
    half = sds(5, 8, 128)
    kept, sent, grads, r0, s = call(
        main_kernel,
        (half, half, sds(9, X, Y, Z), block, block),
        (fields, rows, third, rest, *from_x, *from_r, *inner, *weights),
        [
            pltpu.VMEM((2, len(XLAYERS), YE, ZE), F32),
            pltpu.VMEM((3, X + 6, YE, ZE), F32),
            pltpu.VMEM((X + 4, YE, ZE), F32),
            pltpu.VMEM((X + 2, YE, ZE), F32),
            pltpu.VMEM((10, 8, 128), F32),
        ],
        name="main",
    )
    mine = kept + swap_cores(sent)
    mine = total_over(mine, ("gx", "prop"), 16)
    mine = pairs_sum(mine, "stream", [(0, 1), (2, 3), (4, 5), (6, 7)])
    mine = pairs_sum(mine, "stream", [(1, 2), (3, 4), (5, 6), (7, 0)])
    across = (3, 6, 5, 0, 7, 2, 1, 4)
    both = [(2 * i + c, 2 * across[i] + 1 - c) for i in range(8) for c in range(2)]
    other = swap_cores(mine) + lax.ppermute(mine, ("stream", "core"), both)
    mine = mine + lax.ppermute(mine, "stream", list(enumerate(across)))
    return call(
        final_kernel,
        (sds(3, X, Y, Z), block, sds(3, points)),
        (
            mine,
            other,
            pressure_old,
            grads,
            r0,
            s,
            *weights,
            blade_motion,
            force_coeff.reshape(1, points),
        ),
        [pltpu.VMEM((3, points), F32)],
        name="final",
    )


def solution(mesh):
    cut = Mesh(mesh.devices.reshape(8, 4, 2, 4), ("stream", "gx", "core", "prop"))
    cells = ("stream", ("gx", "core"), "prop")
    placed = (P(None, *cells),) + (P(*cells),) * 4 + (P(),) * 4
    return jax.shard_map(
        shards,
        mesh=cut,
        in_specs=placed,
        out_specs=(P(None, *cells), P(*cells), P()),
        check_vma=False,
    )
```
